256 devices in a mesh: dp: 32 (over x, z), expert: 8 (over y, core).
Axes of the slice: x: 4, y: 4, z: 8, core: 2. Of those that a mesh axis runs over, the one named last changes fastest.
Arguments:
- queries: bfloat16 [512, 6144], P('dp', 'expert'), may hold values from -48 to 48
- new_keys: bfloat16 [512, 1024], P('dp', 'expert'), may hold values from -6 to 6
- new_values: bfloat16 [512, 1024], P('dp', 'expert'), may hold values from -6 to 6
- k_cache: bfloat16 [512, 8, 128, 128], P('dp', 'expert'), may hold values from -48 to 48
- v_cache: bfloat16 [512, 8, 128, 128], P('dp', 'expert'), may hold values from -6 to 6
- lengths: int32 [512], P('dp'), may hold values from 2 to 128, as said below
- residual: bfloat16 [512, 6144], P(None, 'dp'), may hold values from -6 to 6
- w_out: bfloat16 [6144, 6144], P('expert', 'dp'), may hold values from -0.078125 to 0.078125
- router: bfloat16 [6144, 8], replicated, may hold values from -0.078125 to 0.078125
- gain_moe: float32 [6144], replicated, may hold values from 0.5 to 1.5
- w_gate: bfloat16 [8, 6144, 8192], P('expert', None, 'dp'), may hold values from -0.078125 to 0.078125
- w_up: bfloat16 [8, 6144, 8192], P('expert', None, 'dp'), may hold values from -0.078125 to 0.078125
- w_down: bfloat16 [8, 8192, 6144], P('expert', 'dp'), may hold values from -0.0625 to 0.0625
- expert_ids: int32 [512, 2], replicated, may hold values from 0 to 7, all different within a row; in each aligned block of 512 rows (0 to 511, 512 to 1023, ...) at most 256 rows name the same one
- gain_final: float32 [6144], replicated, may hold values from 0.5 to 1.5
- w_vocab: bfloat16 [6144, 32768], P(None, ('dp', 'expert')), may hold values from -12 to 12
- tokens: int32 [512], replicated, may hold values from 0 to 32767
- mu: float32 [512], P(('dp', 'expert')), may hold values from 6 to 12
Outputs:
- hidden_out: bfloat16 [512, 6144], P(('dp', 'expert'))
- surprise: float32 [512], P(('dp', 'expert'))
- mu_next: float32 [512], P(('dp', 'expert'))
The draws below stay inside these ranges and needn't reach their ends.
Inputs may be any that keep to these rules, and one draw needn't show every extreme that they name: `expert_ids`: no expert is named by more than 256 requests, a bound that some block reaches; the two experts of a request differ. `lengths`: some request holds exactly 128 cached positions.
All inputs are finite; a program needn't handle non-finite values.
Results may differ from the reference program's by a relative error of at most 0.008.
Values may be sent and summed in bfloat16 or wider, within the bound.
No kernel may reach another device: no remote copies, remote signals or barrier semaphores. Data moves between devices by JAX's collectives and lax.ppermute only.
A program may use at most 128 MiB of HBM per device.

```python
import math
import jax
import jax.numpy as jnp
import numpy as np
from jax import lax

D = 6144
FF = 8192
HD = 128
LMAX = 128
KVH = 8
HQ = 48
E = 8
VOCAB = 32768
R = 512
CAP = 256


def draw_queries(key, part):
    key = jax.random.fold_in(key, 1)
    base = jnp.clip(jax.random.normal(key, (R, KVH, HQ // KVH, HD)), -6.0, 6.0)
    return base.reshape(R, HQ * HD).astype(jnp.bfloat16)


def draw_k_cache(key, part):
    key = jax.random.fold_in(key, 2)
    base = jnp.clip(jax.random.normal(key, (R, KVH, LMAX, HD)), -6.0, 6.0)
    return base.astype(jnp.bfloat16)


def draw_lengths(key, part):
    key = jax.random.fold_in(key, 3)
    base = jax.random.randint(key, (R,), 2, LMAX + 1)
    where_full = jax.random.randint(jax.random.fold_in(key, 7), (), 0, R)
    return base.at[where_full].set(LMAX).astype(jnp.int32)


def draw_w_vocab(key, part):
    key = jax.random.fold_in(key, 4)
    base = jnp.clip(jax.random.normal(key, (D, VOCAB)), -6.0, 6.0) * (3.0 / D ** 0.5)
    return base.astype(jnp.bfloat16)


def set_ends(values, stream_key, least, top_value):
    spot = [jax.random.randint(jax.random.fold_in(stream_key, axis), (), 0, length) for axis, length in enumerate(values.shape)]
    longest = values.shape.index(max(values.shape))
    next_to = spot[:longest] + [(spot[longest] + 1) % values.shape[longest]] + spot[longest + 1:]
    return values.at[tuple(spot)].set(least).at[tuple(next_to)].set(top_value)


def shard_levels(key, shape, pieces, low, largest):
    factor_of = 1.0
    for axis_at, shards_of in pieces:
        heights = jax.random.uniform(jax.random.fold_in(jax.random.fold_in(key, 6), axis_at), (shards_of,), jnp.float32, low / len(pieces), largest / len(pieces))
        factor_of = factor_of * jnp.repeat(jnp.exp(heights), shape[axis_at] // shards_of).reshape((-1,) + (1,) * (len(shape) - 1 - axis_at))
    return factor_of


def shared_out(key, own, number, rows, number_of, top, reach, skew):
    sequence = jax.random.permutation(key, number_of)
    crowded, ordinary = load_shares(number_of, rows * top, reach, skew, True), load_shares(number_of, rows * top, reach, skew, False)
    places = jnp.arange(number_of)

    def named(tallies, turn):
        used = int((tallies > 0).sum())
        fixed = max(1, used // 4)
        shifted = fixed + (places - fixed + turn * (used - fixed)) % max(1, number_of - fixed)
        return jnp.zeros((number_of,), jnp.int32).at[sequence[jnp.where(places < fixed, places, shifted)]].set(jnp.asarray(tallies, jnp.int32))

    tallies = jnp.where(number % 4 == 0, named(crowded, number // 4), named(ordinary, number - number // 4 - 1))
    mixed = jax.random.permutation(jax.random.fold_in(own, 3), number_of)
    giver, sink = mixed[0:number_of // 2 * 2:2], mixed[1:number_of // 2 * 2:2]
    room = jnp.minimum(tallies[giver] - 1, reach - tallies[sink]) // 2
    room = jnp.where((giver == sequence[0]) | (sink == sequence[0]) | (tallies[sink] == 0), 0, jnp.maximum(room, 0))
    shifted = jax.random.randint(jax.random.fold_in(own, 4), (number_of // 2,), 0, 1 << 20) % (room + 1)
    tallies = tallies.at[giver].add(-shifted).at[sink].add(shifted)
    labels = jnp.searchsorted(jnp.cumsum(tallies), jnp.arange(rows * top), side="right").astype(jnp.int32)
    listing = labels.reshape(top, rows).T
    listing = listing[jax.random.permutation(jax.random.fold_in(own, 1), rows)]
    turn = jax.random.randint(jax.random.fold_in(own, 2), (rows, 1), 0, top)
    return jnp.take_along_axis(listing, (jnp.arange(top)[None, :] + turn) % top, axis=1)


def load_shares(count, total, reach, lean, full):
    portions = [(1 << 20) // math.isqrt(rank ** lean) + 1 for rank in range(1, count + 1)]
    largest = reach if full else min(reach, max(-(-total // count), total * portions[0] // sum(portions)))
    least = 1 if total - largest >= count - 1 else 0
    holding, spare = [largest] + [least] * (count - 1), total - largest - least * (count - 1)
    while spare > 0:
        candidates = [i for i in range(1, count) if holding[i] < largest] or [i for i in range(1, count) if holding[i] < reach]
        mass, remaining = sum([portions[i] for i in candidates]), spare
        for i in candidates:
            addition = min(reach - holding[i], max(1, remaining * portions[i] // mass), spare)
            holding[i] = holding[i] + addition
            spare = spare - addition
    return np.array(holding)


def bell_draw(rng, dims, scale, limit, pieces=(), held_as=jnp.bfloat16):
    result = jax.random.normal(rng, dims, jnp.float32) * scale
    if len(pieces) > 0:
        result = shard_levels(rng, dims, pieces, -0.22, 0.18) * result
    return jnp.clip(result, min=-limit, max=limit).astype(held_as)


def setup_inputs(seed: int = 0) -> dict:
    keys = jax.random.split(jax.random.key(seed), 19)
    queries = draw_queries(jax.random.fold_in(keys[18], 71), 0)
    new_keys = bell_draw(keys[1], (R, KVH * HD), 1.0, 6.0, ((0, 32), (1, 8)))
    new_values = bell_draw(keys[2], (R, KVH * HD), 1.0, 6.0, ((0, 32), (1, 8)))
    k_cache = draw_k_cache(jax.random.fold_in(keys[18], 71), 0)
    v_cache = bell_draw(keys[4], (R, KVH, LMAX, HD), 1.0, 6.0, ((0, 32), (1, 8)))
    lengths = draw_lengths(jax.random.fold_in(keys[18], 71), 0)
    residual = bell_draw(keys[6], (R, D), 1.0, 6.0, ((1, 32),))
    w_out = bell_draw(keys[7], (HQ * HD, D), (HQ * HD) ** -0.5, 0.078125, ((0, 8), (1, 32)))
    router = bell_draw(keys[8], (D, E), D ** -0.5, 0.078125)
    gain_moe = jnp.clip(1.0 + 0.1 * jax.random.normal(keys[9], (D,), jnp.float32), 0.5, 1.5)
    w_gate = bell_draw(keys[10], (E, D, FF), D ** -0.5, 0.078125, ((0, 8), (2, 32)))
    w_up = bell_draw(keys[11], (E, D, FF), D ** -0.5, 0.078125, ((0, 8), (2, 32)))
    w_down = bell_draw(keys[12], (E, FF, D), FF ** -0.5, 0.0625, ((0, 8), (1, 32)))
    expert_ids_keys = jax.random.split(jax.random.fold_in(keys[13], 1), R // R)
    expert_ids_turns = jax.random.permutation(jax.random.fold_in(keys[13], 3), R // R)
    expert_ids = jax.vmap(lambda own, number: shared_out(jax.random.fold_in(keys[13], 2), own, number, R, E, 2, CAP, 2))(expert_ids_keys, expert_ids_turns).reshape((R, 2))
    gain_final = jnp.clip(1.0 + 0.1 * jax.random.normal(keys[14], (D,), jnp.float32), 0.5, 1.5)
    w_vocab = draw_w_vocab(jax.random.fold_in(keys[18], 71), 0)
    tokens = set_ends(jax.random.randint(keys[16], (R,), 0, VOCAB), jax.random.fold_in(keys[16], 1), 0, VOCAB - 1).astype(jnp.int32)
    mu = jnp.clip(6.0 + 6.0 * jax.random.uniform(keys[17], (R,), jnp.float32) ** shard_levels(keys[17], (R,), ((0, 256),), -0.2, 0.2), 6.0, 12.0)
    return dict(queries=queries, new_keys=new_keys, new_values=new_values, k_cache=k_cache, v_cache=v_cache, lengths=lengths, residual=residual, w_out=w_out, router=router, gain_moe=gain_moe, w_gate=w_gate, w_up=w_up, w_down=w_down, expert_ids=expert_ids, gain_final=gain_final, w_vocab=w_vocab, tokens=tokens, mu=mu)


EPS = 1e-05
TARGET = 5.0
RATE = 0.1
LOG_TWO = 0.6931471805599453

def attend(queries, new_keys, new_values, k_cache, v_cache, lengths):
    rows, heads_kv, span, width = k_cache.shape
    group = queries.shape[1] // (heads_kv * width)
    query = queries.astype(jnp.float32).reshape(rows, heads_kv, group, width)
    scale = width ** (-0.5)
    cached = jnp.einsum('rkgd,rkld->rkgl', query, k_cache.astype(jnp.float32)) * scale
    fresh_key = new_keys.astype(jnp.float32).reshape(rows, heads_kv, width)
    fresh = jnp.einsum('rkgd,rkd->rkg', query, fresh_key) * scale
    live = jnp.arange(span, dtype=jnp.int32)[None, :] < lengths[:, None]
    cached = jnp.where(live[:, None, None, :], cached, -1e+30)
    top = jnp.maximum(lax.optimization_barrier(jnp.max(cached, axis=-1)), fresh)
    part_cached = jnp.exp(cached - top[..., None])
    part_fresh = jnp.exp(fresh - top)
    total = lax.optimization_barrier(jnp.sum(part_cached, axis=-1)) + part_fresh
    weight_cached = (part_cached / total[..., None]).astype(jnp.bfloat16)
    weight_fresh = (part_fresh / total).astype(jnp.bfloat16)
    fresh_value = new_values.astype(jnp.float32).reshape(rows, heads_kv, 1, width)
    out = jnp.einsum('rkgl,rkld->rkgd', weight_cached.astype(jnp.float32), v_cache.astype(jnp.float32))
    out = out + weight_fresh.astype(jnp.float32)[..., None] * fresh_value
    return out.reshape(rows, group * heads_kv * width).astype(jnp.bfloat16)

def reference(queries, new_keys, new_values, k_cache, v_cache, lengths, residual, w_out, router, gain_moe, w_gate, w_up, w_down, expert_ids, gain_final, w_vocab, tokens, mu):
    attended = attend(queries, new_keys, new_values, k_cache, v_cache, lengths)
    hidden = (residual.astype(jnp.float32) + jnp.dot(attended, w_out, preferred_element_type=jnp.float32)).astype(jnp.bfloat16)
    hidden_f = hidden.astype(jnp.float32)
    scale_moe = lax.rsqrt(lax.optimization_barrier(jnp.mean(hidden_f * hidden_f, axis=1)) + EPS)
    moe_in = (hidden_f * gain_moe[None, :]).astype(jnp.bfloat16)
    logits_route = scale_moe[:, None] * jnp.dot(moe_in, router, preferred_element_type=jnp.float32)
    first = expert_ids[:, 0]
    second = expert_ids[:, 1]
    first_logit = jnp.take_along_axis(logits_route, first[:, None], axis=1)[:, 0]
    second_logit = jnp.take_along_axis(logits_route, second[:, None], axis=1)[:, 0]
    first_weight = 1.0 / (1.0 + jnp.exp(second_logit - first_logit))
    second_weight = 1.0 / (1.0 + jnp.exp(first_logit - second_logit))
    total = jnp.zeros((R, D), jnp.float32)
    positions = jnp.arange(R, dtype=jnp.int32)
    for expert in range(E):
        hit = (first == expert) | (second == expert)
        slot = jnp.cumsum(hit.astype(jnp.int32)) - 1
        order = jnp.zeros((CAP,), jnp.int32).at[jnp.where(hit, slot, CAP)].set(positions, mode='drop')
        valid = (jnp.arange(CAP, dtype=jnp.int32) < jnp.sum(hit.astype(jnp.int32))).astype(jnp.float32)
        weight = jnp.where(first == expert, first_weight, jnp.where(second == expert, second_weight, 0.0))
        picked = moe_in[order]
        row_scale = scale_moe[order][:, None]
        gate = row_scale * jnp.dot(picked, w_gate[expert], preferred_element_type=jnp.float32)
        up = row_scale * jnp.dot(picked, w_up[expert], preferred_element_type=jnp.float32)
        act = (jax.nn.silu(gate) * up).astype(jnp.bfloat16)
        out = jnp.dot(act, w_down[expert], preferred_element_type=jnp.float32)
        total = total.at[order].add((weight[order] * valid)[:, None] * out)
    hidden_out = (hidden_f + total).astype(jnp.bfloat16)
    out_f = hidden_out.astype(jnp.float32)
    scale_final = lax.rsqrt(lax.optimization_barrier(jnp.mean(out_f * out_f, axis=1)) + EPS)
    final = (out_f * scale_final[:, None] * gain_final[None, :]).astype(jnp.bfloat16)
    logits = jnp.dot(final, w_vocab, preferred_element_type=jnp.float32)
    top = lax.optimization_barrier(jnp.max(logits, axis=1))
    summed = lax.optimization_barrier(jnp.sum(jnp.exp(logits - top[:, None]), axis=1))
    chosen = jnp.take_along_axis(logits, tokens[:, None], axis=1)[:, 0]
    surprise = (top + jnp.log(summed) - chosen) / LOG_TWO
    mu_next = mu - RATE * (surprise - TARGET)
    return (hidden_out, surprise, mu_next)
```

```python
import jax
import jax.numpy as jnp
from jax import lax
from jax.experimental import pallas as pl
from jax.experimental.pallas import tpu as pltpu
from jax.sharding import Mesh
from jax.sharding import PartitionSpec as P

EPS = 1e-05
TARGET = 5.0
RATE = 0.1
LOG_TWO = 0.6931471805599453
F32 = jnp.float32
BF16 = jnp.bfloat16
NX, NZ, NY, NC = 4, 8, 4, 2
NXY = NX * NY
XY = ("x", "y")
EX = ("y", "c")
ALL = ("x", "z", "y", "c")


def swap_cores(value):
    return lax.ppermute(value, "c", [(0, 1), (1, 0)])


def exchange(value, axes):
    return lax.all_to_all(value, axes, split_axis=0, concat_axis=0, tiled=True)


def spread(value, axes, count):
    return exchange(jnp.broadcast_to(value[None], (count,) + value.shape), axes)


def attend(queries, new_keys, new_values, k_cache, v_cache, lengths):
    rows, heads_kv, span, width = k_cache.shape
    group = queries.shape[1] // (heads_kv * width)
    query = queries.reshape(rows, heads_kv, group, width)
    scale = width ** (-0.5)
    cached = (
        jnp.einsum("rkgd,rkld->rkgl", query, k_cache, preferred_element_type=F32) * scale
    )
    fresh_key = new_keys.reshape(rows, heads_kv, width)
    fresh = jnp.einsum("rkgd,rkd->rkg", query, fresh_key, preferred_element_type=F32) * scale
    live = jnp.arange(span, dtype=jnp.int32)[None, :] < lengths[:, None]
    cached = jnp.where(live[:, None, None, :], cached, -1e30)
    top = jnp.maximum(jnp.max(cached, axis=-1), fresh)
    part_cached = jnp.exp(cached - top[..., None])
    part_fresh = jnp.exp(fresh - top)
    total = jnp.sum(part_cached, axis=-1) + part_fresh
    weight_cached = (part_cached / total[..., None]).astype(BF16)
    weight_fresh = (part_fresh / total).astype(BF16)
    fresh_value = new_values.reshape(rows, heads_kv, 1, width).astype(F32)
    out = jnp.einsum("rkgl,rkld->rkgd", weight_cached, v_cache, preferred_element_type=F32)
    out = out + weight_fresh.astype(F32)[..., None] * fresh_value
    return out.reshape(rows, group * heads_kv * width).astype(BF16)


def expert_kernel(
    place, own, other, gate_w, up_w, router_w, gain, ids, act, gate_sum, up_sum, route_sum, squares
):
    step = pl.program_id(0)
    width = own.shape[-1]
    half = own.shape[0] * own.shape[2]
    hidden = jnp.concatenate(
        [own[...].reshape(half, width), other[...].reshape(half, width)], axis=0
    ).astype(F32)
    scaled = (hidden * gain[0]).astype(BF16)
    gate = jnp.dot(scaled, gate_w[...].reshape(width, -1), preferred_element_type=F32)
    up = jnp.dot(scaled, up_w[...].reshape(width, -1), preferred_element_type=F32)
    route = lax.dot_general(
        scaled, router_w[0], (((1,), (1,)), ((), ())), preferred_element_type=F32
    )
    square = jnp.sum(hidden * hidden, axis=1, keepdims=True)

    @pl.when(step == 0)
    def _():
        gate_sum[...] = gate
        up_sum[...] = up
        route_sum[...] = route
        squares[...] = square

    @pl.when(step > 0)
    def _():
        gate_sum[...] += gate
        up_sum[...] += up
        route_sum[...] += route
        squares[...] += square

    @pl.when(step == pl.num_programs(0) - 1)
    def _():
        expert = place[0]
        scale = lax.rsqrt(squares[...] / (width * NZ) + EPS)
        logits = route_sum[...] * scale
        lanes = lax.broadcasted_iota(jnp.int32, logits.shape, 1)
        first = ids[:, 0:1]
        second = ids[:, 1:2]
        first_logit = jnp.sum(jnp.where(lanes == first, logits, 0.0), axis=1, keepdims=True)
        second_logit = jnp.sum(jnp.where(lanes == second, logits, 0.0), axis=1, keepdims=True)
        is_first = first == expert
        gap = second_logit - first_logit
        weight = 1.0 / (1.0 + jnp.exp(jnp.where(is_first, gap, -gap)))
        weight = jnp.where(is_first | (second == expert), weight, 0.0)
        gated = gate_sum[...] * scale
        value = jax.nn.silu(gated) * (up_sum[...] * scale)
        act[...] = (weight * value).astype(BF16)


def experts(place, own, other, gate_w, up_w, router_w, gain, ids):
    _, _, rows, width = own.shape
    total = 2 * NXY * rows
    hidden_units = gate_w.shape[-1]
    unit = width // NX
    block = pl.BlockSpec((NXY, 1, rows, width), lambda z, p: (0, z, 0, 0))
    weights = pl.BlockSpec((NX, 1, unit, hidden_units), lambda z, p: (0, z, 0, 0))
    count = router_w.shape[1]
    return pl.pallas_call(
        expert_kernel,
        out_shape=jax.ShapeDtypeStruct((total, hidden_units), BF16),
        grid_spec=pltpu.PrefetchScalarGridSpec(
            num_scalar_prefetch=1,
            grid=(NZ,),
            in_specs=[
                block,
                block,
                weights,
                weights,
                pl.BlockSpec((1, count, width), lambda z, p: (z, 0, 0)),
                pl.BlockSpec((1, 1, width), lambda z, p: (z, 0, 0)),
                pl.BlockSpec((total, 2), lambda z, p: (0, 0)),
            ],
            out_specs=pl.BlockSpec((total, hidden_units), lambda z, p: (0, 0)),
            scratch_shapes=[
                pltpu.VMEM((total, hidden_units), F32),
                pltpu.VMEM((total, hidden_units), F32),
                pltpu.VMEM((total, count), F32),
                pltpu.VMEM((total, 1), F32),
            ],
        ),
        compiler_params=pltpu.CompilerParams(
            dimension_semantics=("arbitrary",), vmem_limit_bytes=48 << 20
        ),
        cost_estimate=pl.CostEstimate(
            flops=2 * total * width * NZ * 2 * hidden_units,
            bytes_accessed=13 << 20,
            transcendentals=total * hidden_units,
        ),
        name="experts",
    )(
        place,
        own,
        other,
        gate_w.reshape(NX, NZ, unit, hidden_units),
        up_w.reshape(NX, NZ, unit, hidden_units),
        router_w,
        gain,
        ids,
    )


def down_kernel(place, mine, theirs, w_mine, w_theirs, out):
    half = mine.shape[0] // 2
    rows = half // NXY
    width = out.shape[-1]
    core = place[1]
    for part in range(2):
        here = mine[part * half : (part + 1) * half, :]
        there = theirs[(1 - part) * half : (2 - part) * half, :]
        total = jnp.dot(here, w_mine[...], preferred_element_type=F32)
        total += jnp.dot(there, w_theirs[...], preferred_element_type=F32)
        start = pl.multiple_of((core if part == 0 else 1 - core) * rows, rows)
        out[:, 0, pl.ds(start, rows), :] = total.astype(BF16).reshape(NXY, rows, width)


def down(place, mine, theirs, w_mine, w_theirs):
    total, units = mine.shape
    width = w_theirs.shape[1] // NZ
    rows = total // NXY
    return pl.pallas_call(
        down_kernel,
        out_shape=jax.ShapeDtypeStruct((NXY, NZ, rows, width), BF16),
        grid_spec=pltpu.PrefetchScalarGridSpec(
            num_scalar_prefetch=1,
            grid=(NZ,),
            in_specs=[
                pl.BlockSpec((total, units), lambda z, p: (0, 0)),
                pl.BlockSpec((total, units), lambda z, p: (0, 0)),
                pl.BlockSpec((units, width), lambda z, p: (0, p[1] * NZ + z)),
                pl.BlockSpec((units, width), lambda z, p: (0, z)),
            ],
            out_specs=pl.BlockSpec((NXY, 1, rows, width), lambda z, p: (0, z, 0, 0)),
        ),
        compiler_params=pltpu.CompilerParams(
            dimension_semantics=("arbitrary",), vmem_limit_bytes=48 << 20
        ),
        cost_estimate=pl.CostEstimate(
            flops=2 * total * units * 2 * width * NZ, bytes_accessed=7 << 20, transcendentals=0
        ),
        name="down",
    )(place, mine, theirs, w_mine, w_theirs)


def head_kernel(place, own, other, weights, gain, token, stats, acc, squares):
    step = pl.program_id(0)
    width = own.shape[-1]
    total = acc.shape[0]

    @pl.when(step == 0)
    def _():
        acc[...] = jnp.zeros_like(acc)
        squares[...] = jnp.zeros_like(squares)

    def add(block):
        hidden = block[...].reshape(total, width).astype(F32)
        scaled = (hidden * gain[0]).astype(BF16)
        acc[...] += jnp.dot(scaled, weights[...], preferred_element_type=F32)
        squares[...] += jnp.sum(hidden * hidden, axis=1, keepdims=True)

    @pl.when(step < NZ)
    def _():
        add(own)

    @pl.when(step >= NZ)
    def _():
        add(other)

    @pl.when(step == pl.num_programs(0) - 1)
    def _():
        logits = acc[...] * lax.rsqrt(squares[...] / (width * NZ * NC) + EPS)
        lanes = lax.broadcasted_iota(jnp.int32, logits.shape, 1)
        top = jnp.max(logits, axis=1, keepdims=True)
        summed = jnp.sum(jnp.exp(logits - top), axis=1, keepdims=True)
        local = token[...] - place[2] * logits.shape[1]
        chosen = jnp.sum(jnp.where(lanes == local, logits, 0.0), axis=1, keepdims=True)
        stats[...] = jnp.where(lanes == 0, top, jnp.where(lanes == 1, summed, chosen))


def head(place, own, other, w_vocab, gain, token):
    _, _, rows, width = own.shape
    total = NXY * rows
    vocab = w_vocab.shape[1]

    def at(s, p):
        flip = s // NZ
        return (p[1] + flip - 2 * p[1] * flip) * NZ + s % NZ

    return pl.pallas_call(
        head_kernel,
        out_shape=jax.ShapeDtypeStruct((total, vocab), F32),
        grid_spec=pltpu.PrefetchScalarGridSpec(
            num_scalar_prefetch=1,
            grid=(NC * NZ,),
            in_specs=[
                pl.BlockSpec(
                    (NXY, 1, rows, width), lambda s, p: (0, jnp.minimum(s, NZ - 1), 0, 0)
                ),
                pl.BlockSpec(
                    (NXY, 1, rows, width), lambda s, p: (0, jnp.maximum(s - NZ, 0), 0, 0)
                ),
                pl.BlockSpec((width, vocab), lambda s, p: (at(s, p), 0)),
                pl.BlockSpec((1, 1, width), lambda s, p: (at(s, p), 0, 0)),
                pl.BlockSpec((total, 1), lambda s, p: (0, 0)),
            ],
            out_specs=pl.BlockSpec((total, vocab), lambda s, p: (0, 0)),
            scratch_shapes=[pltpu.VMEM((total, vocab), F32), pltpu.VMEM((total, 1), F32)],
        ),
        compiler_params=pltpu.CompilerParams(
            dimension_semantics=("arbitrary",), vmem_limit_bytes=48 << 20
        ),
        cost_estimate=pl.CostEstimate(
            flops=2 * total * width * NZ * NC * vocab,
            bytes_accessed=8 << 20,
            transcendentals=total * vocab,
        ),
        name="head",
    )(place, own, other, w_vocab, gain, token)


def shards(
    queries,
    new_keys,
    new_values,
    k_cache,
    v_cache,
    lengths,
    residual,
    w_out,
    router,
    gain_moe,
    w_gate,
    w_up,
    w_down,
    expert_ids,
    gain_final,
    w_vocab,
    tokens,
    mu,
):
    x, z, y, core = (lax.axis_index(name) for name in ("x", "z", "y", "c"))
    expert = y * NC + core
    owner = lax.axis_index(ALL)
    place = jnp.stack([expert, core, owner]).astype(jnp.int32)
    width_all = gain_moe.shape[0]
    unit = w_out.shape[1]
    total_rows = residual.shape[0]
    part_rows = total_rows // (NX * NY * NC)

    packs = []
    for shift in range(NX):
        target = (x + shift) % NX
        rows = lax.dynamic_slice_in_dim(
            residual, (target * NY * NC + expert) * part_rows, part_rows
        )
        pack = jnp.concatenate([w_out, rows], axis=0)
        if shift:
            pack = lax.ppermute(pack, "x", [(i, (i + shift) % NX) for i in range(NX)])
        packs.append(pack)
    depth = w_out.shape[0]
    w_wide = jnp.concatenate([pack[:depth] for pack in packs], axis=1)
    residual_wide = jnp.concatenate([pack[depth:] for pack in packs], axis=1)

    half = width_all // NC
    down_sent = lax.dynamic_slice_in_dim(w_down[0], (1 - core) * half, half, axis=1)
    down_other = swap_cores(down_sent)

    attended = attend(queries, new_keys, new_values, k_cache, v_cache, lengths)
    attended_x = spread(attended, "z", NZ).reshape(-1, depth)
    partial_heads = jnp.dot(attended_x, w_wide, preferred_element_type=F32).astype(BF16)
    pieces = exchange(partial_heads.reshape(NY * NC, part_rows, NX * unit), EX)
    summed = jnp.sum(pieces.astype(F32), axis=0) + residual_wide.astype(F32)
    turned = summed.astype(BF16).reshape(part_rows, NX, unit)
    hidden = jnp.concatenate(
        [lax.dynamic_index_in_dim(turned, (x - i) % NX, 1, keepdims=False) for i in range(NX)],
        axis=1,
    )

    hidden_z = spread(hidden, "z", NZ)
    own = spread(hidden_z, XY, NXY)
    other = swap_cores(own)

    order = expert_ids.reshape(NXY, NC, part_rows, 2).transpose(1, 0, 2, 3)
    order = jnp.where(core == 0, order, order[::-1]).reshape(total_rows, 2)
    router_z = router.T.reshape(-1, NX, NZ, unit).transpose(2, 0, 1, 3).reshape(NZ, -1, NX * unit)
    gain_z = gain_moe.reshape(NX, NZ, unit).transpose(1, 0, 2).reshape(NZ, 1, NX * unit)
    act = experts(place, own, other, w_gate[0], w_up[0], router_z, gain_z, order)
    act_other = swap_cores(act)
    sent = down(place, act, act_other, w_down[0], down_other)
    sums = jnp.sum(exchange(sent, XY).astype(F32), axis=0).astype(BF16)
    sums = jnp.sum(exchange(sums, "z").astype(F32), axis=0)

    block_rows = NC * part_rows
    block = half // NZ
    place_xy = x * NY + y
    mine = lax.dynamic_index_in_dim(own, place_xy, 0, keepdims=False)
    theirs = lax.dynamic_index_in_dim(other, place_xy, 0, keepdims=False)
    rows_here = jnp.where(
        core == 0,
        jnp.concatenate([mine, theirs], axis=1),
        jnp.concatenate([theirs, mine], axis=1),
    )
    first_unit = core * (half // unit) + z * (block // unit)
    cut = []
    for i in range(block // unit):
        at = first_unit + i
        slab = lax.dynamic_index_in_dim(rows_here, at % NZ, 0, keepdims=False)
        slab = slab.reshape(block_rows, NX, unit)
        cut.append(lax.dynamic_index_in_dim(slab, at // NZ, 1, keepdims=False))
    hidden_here = jnp.concatenate(cut, axis=1).astype(F32)
    moved = (hidden_here + sums).astype(BF16)

    final_own = spread(spread(moved, "z", NZ), XY, NXY)
    final_other = swap_cores(final_own)
    stats = head(
        place,
        final_own,
        final_other,
        w_vocab,
        gain_final.reshape(NC * NZ, 1, block),
        tokens[:, None],
    )
    own_rows = total_rows // (NX * NZ * NY * NC)
    low = (z % 2) * part_rows + expert * own_rows
    start = (x * NY + z // 2, 0, low, 0)
    size = (1, NZ, own_rows, block)
    near = lax.dynamic_slice(final_own, start, size)[0].transpose(1, 0, 2).reshape(own_rows, half)
    far = lax.dynamic_slice(final_other, start, size)[0].transpose(1, 0, 2).reshape(own_rows, half)
    hidden_out = jnp.where(
        core == 0,
        jnp.concatenate([near, far], axis=1),
        jnp.concatenate([far, near], axis=1),
    )

    flat = stats[:, :4].reshape(-1, own_rows * 4)
    flat = jnp.pad(flat, ((0, 0), (0, 128 - own_rows * 4)))
    got = exchange(flat, ALL)[:, : own_rows * 4].reshape(-1, own_rows, 4)
    top = jnp.max(got[:, :, 0], axis=0)
    summed_all = jnp.sum(got[:, :, 1] * jnp.exp(got[:, :, 0] - top[None]), axis=0)
    chosen = jnp.sum(got[:, :, 2], axis=0)
    surprise = (top + jnp.log(summed_all) - chosen) / LOG_TWO
    mu_next = mu - RATE * (surprise - TARGET)
    return (hidden_out, surprise, mu_next)


def solution(mesh):
    fine = Mesh(mesh.devices.reshape(NX, NZ, NY, NC), ALL)
    dp = ("x", "z")
    return jax.shard_map(
        shards,
        mesh=fine,
        in_specs=(
            P(dp, EX),
            P(dp, EX),
            P(dp, EX),
            P(dp, EX, None, None),
            P(dp, EX, None, None),
            P(dp),
            P(None, dp),
            P(EX, dp),
            P(),
            P(),
            P(EX, None, dp),
            P(EX, None, dp),
            P(EX, dp, None),
            P(),
            P(),
            P(None, ALL),
            P(),
            P(ALL),
        ),
        out_specs=(P(ALL, None), P(ALL), P(ALL)),
        check_vma=False,
    )
```

```python
import jax
import jax.numpy as jnp
from jax import lax
from jax.experimental import pallas as pl
from jax.experimental.pallas import tpu as pltpu
from jax.sharding import Mesh
from jax.sharding import PartitionSpec as P

EPS = 1e-05
TARGET = 5.0
RATE = 0.1
LOG_TWO = 0.6931471805599453
F32 = jnp.float32
BF16 = jnp.bfloat16
NX, NZ, NY, NC = 4, 8, 4, 2
NXY = NX * NY
XY = ("x", "y")
EX = ("y", "c")
ALL = ("x", "z", "y", "c")


def swap_cores(value):
    return lax.ppermute(value, "c", [(0, 1), (1, 0)])


def exchange(value, axes):
    return lax.all_to_all(value, axes, split_axis=0, concat_axis=0, tiled=True)


def spread(value, axes, count):
    return exchange(jnp.broadcast_to(value[None], (count,) + value.shape), axes)


def attend(queries, new_keys, new_values, k_cache, v_cache, lengths):
    rows, heads_kv, span, width = k_cache.shape
    group = queries.shape[1] // (heads_kv * width)
    query = queries.reshape(rows, heads_kv, group, width)
    scale = width ** (-0.5)
    cached = (
        jnp.einsum("rkgd,rkld->rkgl", query, k_cache, preferred_element_type=F32) * scale
    )
    fresh_key = new_keys.reshape(rows, heads_kv, width)
    fresh = jnp.einsum("rkgd,rkd->rkg", query, fresh_key, preferred_element_type=F32) * scale
    live = jnp.arange(span, dtype=jnp.int32)[None, :] < lengths[:, None]
    cached = jnp.where(live[:, None, None, :], cached, -1e30)
    top = jnp.maximum(jnp.max(cached, axis=-1), fresh)
    part_cached = jnp.exp(cached - top[..., None])
    part_fresh = jnp.exp(fresh - top)
    total = jnp.sum(part_cached, axis=-1) + part_fresh
    weight_cached = (part_cached / total[..., None]).astype(BF16)
    weight_fresh = (part_fresh / total).astype(BF16)
    fresh_value = new_values.reshape(rows, heads_kv, 1, width).astype(F32)
    out = jnp.einsum("rkgl,rkld->rkgd", weight_cached, v_cache, preferred_element_type=F32)
    out = out + weight_fresh.astype(F32)[..., None] * fresh_value
    return out.reshape(rows, group * heads_kv * width).astype(BF16)


def expert_kernel(
    place, state, gate_w, up_w, router_w, ids, act, gate_sum, up_sum, route_sum, squares
):
    step = pl.program_id(0)
    width = state.shape[-1]
    hidden = state[...].reshape(-1, width)
    gate = jnp.dot(hidden, gate_w[...].reshape(width, -1), preferred_element_type=F32)
    up = jnp.dot(hidden, up_w[...].reshape(width, -1), preferred_element_type=F32)
    route = lax.dot_general(
        hidden, router_w[0], (((1,), (1,)), ((), ())), preferred_element_type=F32
    )
    wide = hidden.astype(F32)
    square = jnp.zeros(squares.shape, F32)
    for start in range(0, width, 128):
        piece = wide[:, start : start + 128]
        square += piece * piece

    @pl.when(step == 0)
    def _():
        gate_sum[...] = gate
        up_sum[...] = up
        route_sum[...] = route
        squares[...] = square

    @pl.when(step > 0)
    def _():
        gate_sum[...] += gate
        up_sum[...] += up
        route_sum[...] += route
        squares[...] += square

    @pl.when(step == pl.num_programs(0) - 1)
    def _():
        expert = place[0]
        mean = jnp.sum(squares[...], axis=1, keepdims=True) / (width * NZ)
        scale = lax.rsqrt(mean + EPS)
        logits = route_sum[...] * scale
        lanes = lax.broadcasted_iota(jnp.int32, logits.shape, 1)
        first = ids[:, 0:1]
        second = ids[:, 1:2]
        first_logit = jnp.sum(jnp.where(lanes == first, logits, 0.0), axis=1, keepdims=True)
        second_logit = jnp.sum(jnp.where(lanes == second, logits, 0.0), axis=1, keepdims=True)
        is_first = first == expert
        gap = second_logit - first_logit
        weight = 1.0 / (1.0 + jnp.exp(jnp.where(is_first, gap, -gap)))
        weight = jnp.where(is_first | (second == expert), weight, 0.0)
        gated = gate_sum[...] * scale
        value = jax.nn.silu(gated) * (up_sum[...] * scale)
        act[...] = (weight * value).astype(BF16)


def experts(place, state, gate_w, up_w, router_w, ids):
    _, _, rows, width = state.shape
    total = NXY * rows
    hidden_units = gate_w.shape[-1]
    unit = width // NX
    weights = pl.BlockSpec((NX, 1, unit, hidden_units), lambda z, p: (0, z, 0, 0))
    count = router_w.shape[1]
    return pl.pallas_call(
        expert_kernel,
        out_shape=jax.ShapeDtypeStruct((total, hidden_units), BF16),
        grid_spec=pltpu.PrefetchScalarGridSpec(
            num_scalar_prefetch=1,
            grid=(NZ,),
            in_specs=[
                pl.BlockSpec((NXY, 1, rows, width), lambda z, p: (0, z, 0, 0)),
                weights,
                weights,
                pl.BlockSpec((1, count, width), lambda z, p: (z, 0, 0)),
                pl.BlockSpec((total, 2), lambda z, p: (0, 0)),
            ],
            out_specs=pl.BlockSpec((total, hidden_units), lambda z, p: (0, 0)),
            scratch_shapes=[
                pltpu.VMEM((total, hidden_units), F32),
                pltpu.VMEM((total, hidden_units), F32),
                pltpu.VMEM((total, count), F32),
                pltpu.VMEM((total, 128), F32),
            ],
        ),
        compiler_params=pltpu.CompilerParams(
            dimension_semantics=("arbitrary",), vmem_limit_bytes=32 << 20
        ),
        cost_estimate=pl.CostEstimate(
            flops=2 * total * width * NZ * 2 * hidden_units,
            bytes_accessed=10 << 20,
            transcendentals=total * hidden_units,
        ),
        name="experts",
    )(
        place,
        state,
        gate_w.reshape(NX, NZ, unit, hidden_units),
        up_w.reshape(NX, NZ, unit, hidden_units),
        router_w,
        ids,
    )


def down_kernel(
    place, mine_own, mine_other, theirs_own, theirs_other, w_mine, w_theirs, out
):
    width = out.shape[-1]
    core = place[1]
    for mine, theirs, which in (
        (mine_own, theirs_own, core),
        (mine_other, theirs_other, 1 - core),
    ):
        total = jnp.dot(mine[...], w_mine[...], preferred_element_type=F32)
        total += jnp.dot(theirs[...], w_theirs[...], preferred_element_type=F32)
        out[0, :, pl.ds(which, 1), :, :] = total.astype(BF16).reshape(NXY, 1, -1, width)


def down(place, acts, w_mine, w_theirs):
    total, units = acts[0].shape
    rows = total // NXY
    width = w_theirs.shape[1] // NX
    steps = 2
    block = width // steps
    return pl.pallas_call(
        down_kernel,
        out_shape=jax.ShapeDtypeStruct((NX, NXY, NC, rows, width), BF16),
        grid_spec=pltpu.PrefetchScalarGridSpec(
            num_scalar_prefetch=1,
            grid=(NX, steps),
            in_specs=[pl.BlockSpec((total, units), lambda x, s, p: (0, 0))] * 4
            + [
                pl.BlockSpec((units, block), lambda x, s, p: (0, (p[1] * NX + x) * steps + s)),
                pl.BlockSpec((units, block), lambda x, s, p: (0, x * steps + s)),
            ],
            out_specs=pl.BlockSpec(
                (1, NXY, NC, rows, block), lambda x, s, p: (x, 0, 0, 0, s)
            ),
        ),
        compiler_params=pltpu.CompilerParams(
            dimension_semantics=("arbitrary", "arbitrary"), vmem_limit_bytes=32 << 20
        ),
        cost_estimate=pl.CostEstimate(
            flops=8 * total * units * width * NX, bytes_accessed=7 << 20, transcendentals=0
        ),
        name="down",
    )(place, *acts, w_mine, w_theirs)


def head_kernel(own, other, w_own, w_other, out):
    width = own.shape[-1]
    vocab = w_own.shape[1]
    rows = out.shape[1]
    near = own[...].reshape(-1, width)
    far = other[...].reshape(-1, width)
    logits = jnp.dot(near, w_own[...], preferred_element_type=F32)
    logits += jnp.dot(far, w_other[...], preferred_element_type=F32)
    square = jnp.zeros((near.shape[0], 128), F32)
    for part in (near.astype(F32), far.astype(F32)):
        for start in range(0, width, 128):
            piece = part[:, start : start + 128]
            square += piece * piece
    square = jnp.sum(square, axis=1, keepdims=True)
    high = square.astype(BF16).astype(F32)
    lanes = lax.broadcasted_iota(jnp.int32, (near.shape[0], 128), 1)
    extra = jnp.where(lanes == 0, high, jnp.where(lanes == 1, square - high, 0.0))
    count = near.shape[0] // NX
    out[:, :count, :vocab] = logits.astype(BF16).reshape(NX, count, vocab)
    out[:, :count, vocab:] = extra.astype(BF16).reshape(NX, count, 128)
    out[:, count:, :] = jnp.zeros((NX, rows - count, vocab + 128), BF16)


def head(own, other, w_own, w_other, rows):
    vocab = w_own.shape[1]
    total = own.shape[0] * own.shape[1] * own.shape[2]
    return pl.pallas_call(
        head_kernel,
        out_shape=jax.ShapeDtypeStruct((NX, rows, vocab + 128), BF16),
        compiler_params=pltpu.CompilerParams(vmem_limit_bytes=32 << 20),
        cost_estimate=pl.CostEstimate(
            flops=4 * total * own.shape[3] * vocab, bytes_accessed=4 << 20, transcendentals=0
        ),
        name="head",
    )(own, other, w_own, w_other)


def finish_kernel(place, parts, token, stats):
    count = token.shape[0]
    vocab = parts.shape[2] - 128
    total = jnp.sum(parts[:, :count, :].astype(F32), axis=0)
    square = jnp.sum(total[:, vocab:], axis=1, keepdims=True)
    logits = total[:, :vocab] * lax.rsqrt(square / place[1] + EPS)
    top = jnp.max(logits, axis=1, keepdims=True)
    summed = jnp.sum(jnp.exp(logits - top), axis=1, keepdims=True)
    slice_width = vocab // NX
    local = token[...] - place[0] * slice_width
    block = NZ * NY * NC * slice_width
    lanes = lax.broadcasted_iota(jnp.int32, logits.shape, 1)
    entry = (lanes // slice_width) * block + lanes % slice_width
    chosen = jnp.sum(jnp.where(entry == local, logits, 0.0), axis=1, keepdims=True)
    lane = lax.broadcasted_iota(jnp.int32, stats.shape, 1)
    stats[...] = jnp.where(lane == 0, top, jnp.where(lane == 1, summed, chosen))


def finish(place, parts, token):
    return pl.pallas_call(
        finish_kernel,
        out_shape=jax.ShapeDtypeStruct((token.shape[0], 128), F32),
        in_specs=[
            pl.BlockSpec(memory_space=pltpu.SMEM),
            pl.BlockSpec(memory_space=pltpu.VMEM),
            pl.BlockSpec(memory_space=pltpu.VMEM),
        ],
        compiler_params=pltpu.CompilerParams(vmem_limit_bytes=32 << 20),
        name="finish",
    )(place, parts, token)


def shards(
    queries,
    new_keys,
    new_values,
    k_cache,
    v_cache,
    lengths,
    residual,
    w_out,
    router,
    gain_moe,
    w_gate,
    w_up,
    w_down,
    expert_ids,
    gain_final,
    w_vocab,
    tokens,
    mu,
):
    x, z, y, core = (lax.axis_index(name) for name in ("x", "z", "y", "c"))
    expert = y * NC + core
    place = jnp.stack([expert, core]).astype(jnp.int32)
    width_all = gain_moe.shape[0]
    unit = w_out.shape[1]
    total_rows = residual.shape[0]
    part_rows = total_rows // (NX * NY * NC)

    packs = []
    for shift in range(NX):
        target = (x + shift) % NX
        rows = lax.dynamic_slice_in_dim(
            residual, (target * NY * NC + expert) * part_rows, part_rows
        )
        pack = jnp.concatenate([w_out, rows], axis=0)
        if shift:
            pack = lax.ppermute(pack, "x", [(i, (i + shift) % NX) for i in range(NX)])
        packs.append(pack)
    depth = w_out.shape[0]
    w_wide = jnp.concatenate([pack[:depth] for pack in packs], axis=1)
    residual_wide = jnp.concatenate([pack[depth:] for pack in packs], axis=1)

    half = width_all // NC
    slab = half // NX
    vocab_rows = w_vocab.reshape(NC, NX, slab, -1)
    vocab_parts = []
    for shift in range(NX):
        part = lax.dynamic_index_in_dim(vocab_rows, (x + shift) % NX, 1, keepdims=False)
        if shift:
            part = lax.ppermute(part, "x", [(i, (i + shift) % NX) for i in range(NX)])
        vocab_parts.append(part)
    gain_slab = gain_final.reshape(NC, NX, slab)
    gain_slab = lax.dynamic_index_in_dim(gain_slab, x, 1, keepdims=False)[:, :, None]
    columns = []
    for i in range(NX):
        away = (x - i) % NX
        part = vocab_parts[NX - 1]
        for shift in range(NX - 1):
            part = jnp.where(away == shift, vocab_parts[shift], part)
        columns.append((part.astype(F32) * gain_slab).astype(BF16))
    head_w = jnp.concatenate(columns, axis=2)
    head_own = lax.dynamic_index_in_dim(head_w, core, 0, keepdims=False)
    head_other = lax.dynamic_index_in_dim(head_w, 1 - core, 0, keepdims=False)

    down_sent = lax.dynamic_slice_in_dim(w_down[0], (1 - core) * half, half, axis=1)
    down_other = swap_cores(down_sent)

    attended = attend(queries, new_keys, new_values, k_cache, v_cache, lengths)
    attended_x = spread(attended, "z", NZ).reshape(-1, depth)
    partial_heads = jnp.dot(attended_x, w_wide, preferred_element_type=F32).astype(BF16)
    pieces = exchange(partial_heads.reshape(NY * NC, part_rows, NX * unit), EX)
    summed = jnp.sum(pieces.astype(F32), axis=0) + residual_wide.astype(F32)
    turned = summed.astype(BF16).reshape(part_rows, NX, unit)
    hidden = jnp.concatenate(
        [lax.dynamic_index_in_dim(turned, (x - i) % NX, 1, keepdims=False) for i in range(NX)],
        axis=1,
    )

    hidden_z = spread(hidden, "z", NZ)
    own = spread(hidden_z, XY, NXY)
    other = swap_cores(own)

    order = expert_ids.reshape(NXY, NC, part_rows, 2).transpose(1, 0, 2, 3)
    order = order.reshape(NC, -1, 2)
    order_own = lax.dynamic_index_in_dim(order, core, 0, keepdims=False)
    order_other = lax.dynamic_index_in_dim(order, 1 - core, 0, keepdims=False)
    gain_col = gain_moe[:, None]
    router_g = (router.astype(F32) * gain_col).astype(BF16)
    router_z = router_g.T.reshape(-1, NX, NZ, unit).transpose(2, 0, 1, 3)
    router_z = router_z.reshape(NZ, -1, NX * unit)
    gate_g = (w_gate[0].astype(F32) * gain_col).astype(BF16)
    up_g = (w_up[0].astype(F32) * gain_col).astype(BF16)
    act_own = experts(place, own, gate_g, up_g, router_z, order_own)
    act_other = experts(place, other, gate_g, up_g, router_z, order_other)
    acts = (act_own, act_other, swap_cores(act_other), swap_cores(act_own))
    sent = down(place, acts, w_down[0], down_other)
    sent = sent.reshape(NXY, NZ, part_rows, slab)
    sums = jnp.sum(exchange(sent, XY).astype(F32), axis=0).astype(BF16)
    sums = jnp.sum(exchange(sums, "z").astype(F32), axis=0)

    units = slab // unit
    first_unit = core * (half // unit) + x * units
    start = (y * NX + z // 2, first_unit % NZ, 0, 0)
    size = (1, units, part_rows, NX * unit)
    rows_here = jnp.where(
        z % 2 == core, lax.dynamic_slice(own, start, size), lax.dynamic_slice(other, start, size)
    )[0].reshape(units, part_rows, NX, unit)
    cut = lax.dynamic_index_in_dim(rows_here, first_unit // NZ, 2, keepdims=False)
    hidden_here = cut.transpose(1, 0, 2).reshape(part_rows, slab).astype(F32)
    moved = (hidden_here + sums).astype(BF16)

    final_own = spread(spread(moved, "z", NZ), "y", NY).reshape(NY, NZ, part_rows, slab)
    final_other = swap_cores(final_own)
    count = total_rows // NX
    partial = head(final_own, final_other, head_own, head_other, count + 16)

    own_rows = total_rows // (NX * NZ * NY * NC)
    size = (NX, 1, own_rows, slab)
    start = (0, z, expert * own_rows, 0)
    near = lax.dynamic_slice(final_own, start, size)
    far = lax.dynamic_slice(final_other, start, size)
    low = jnp.where(core == 0, near, far)
    high = jnp.where(core == 0, far, near)
    vocab = head_own.shape[1]
    rows_out = jnp.concatenate([low, high], axis=1).reshape(NX, -1, vocab)
    partial = lax.dynamic_update_slice(partial, rows_out, (0, count, 0))
    parts = exchange(partial, "x")
    hidden_out = parts[:, count : count + rows_out.shape[1], :vocab]
    hidden_out = hidden_out.reshape(NX, NC, own_rows, slab).transpose(2, 1, 0, 3)
    hidden_out = hidden_out.reshape(own_rows, width_all)

    token = lax.dynamic_slice_in_dim(tokens, x * count, count)[:, None]
    where = jnp.stack([z * (NY * NC) + expert, jnp.int32(width_all)]).astype(jnp.int32)
    stats = finish(where, parts, token)
    flat = stats[:, :4].reshape(-1, own_rows * 4)
    flat = jnp.pad(flat, ((0, 0), (0, 128 - own_rows * 4)))
    got = exchange(flat, ("z", "y", "c"))[:, : own_rows * 4].reshape(-1, own_rows, 4)
    top = jnp.max(got[:, :, 0], axis=0)
    summed_all = jnp.sum(got[:, :, 1] * jnp.exp(got[:, :, 0] - top[None]), axis=0)
    chosen = jnp.sum(got[:, :, 2], axis=0)
    surprise = (top + jnp.log(summed_all) - chosen) / LOG_TWO
    mu_next = mu - RATE * (surprise - TARGET)
    return (hidden_out, surprise, mu_next)


def solution(mesh):
    fine = Mesh(mesh.devices.reshape(NX, NZ, NY, NC), ALL)
    dp = ("x", "z")
    return jax.shard_map(
        shards,
        mesh=fine,
        in_specs=(
            P(dp, EX),
            P(dp, EX),
            P(dp, EX),
            P(dp, EX, None, None),
            P(dp, EX, None, None),
            P(dp),
            P(None, dp),
            P(EX, dp),
            P(),
            P(),
            P(EX, None, dp),
            P(EX, None, dp),
            P(EX, dp, None),
            P(),
            P(),
            P(None, ALL),
            P(),
            P(ALL),
        ),
        out_specs=(P(ALL, None), P(ALL), P(ALL)),
        check_vma=False,
    )
```

```python
import jax
import jax.numpy as jnp
from jax import lax
from jax.experimental import pallas as pl
from jax.experimental.pallas import tpu as pltpu
from jax.sharding import Mesh
from jax.sharding import PartitionSpec as P

EPS = 1e-05
TARGET = 5.0
RATE = 0.1
LOG_TWO = 0.6931471805599453
F32 = jnp.float32
BF16 = jnp.bfloat16
NX, NZ, NY, NC = 4, 8, 4, 2
NXY = NX * NY
XY = ("x", "y")
EX = ("y", "c")
ALL = ("x", "z", "y", "c")


def swap_cores(value):
    return lax.ppermute(value, "c", [(0, 1), (1, 0)])


def exchange(value, axes):
    return lax.all_to_all(value, axes, split_axis=0, concat_axis=0, tiled=True)


def spread(value, axes, count):
    return exchange(jnp.broadcast_to(value[None], (count,) + value.shape), axes)


def attend(queries, new_keys, new_values, k_cache, v_cache, lengths):
    rows, heads_kv, span, width = k_cache.shape
    group = queries.shape[1] // (heads_kv * width)
    query = queries.reshape(rows, heads_kv, group, width)
    scale = width ** (-0.5)
    cached = (
        jnp.einsum("rkgd,rkld->rkgl", query, k_cache, preferred_element_type=F32) * scale
    )
    fresh_key = new_keys.reshape(rows, heads_kv, width)
    fresh = jnp.einsum("rkgd,rkd->rkg", query, fresh_key, preferred_element_type=F32) * scale
    live = jnp.arange(span, dtype=jnp.int32)[None, :] < lengths[:, None]
    cached = jnp.where(live[:, None, None, :], cached, -1e30)
    top = jnp.maximum(jnp.max(cached, axis=-1), fresh)
    part_cached = jnp.exp(cached - top[..., None])
    part_fresh = jnp.exp(fresh - top)
    total = jnp.sum(part_cached, axis=-1) + part_fresh
    weight_cached = (part_cached / total[..., None]).astype(BF16)
    weight_fresh = (part_fresh / total).astype(BF16)
    fresh_value = new_values.reshape(rows, heads_kv, 1, width).astype(F32)
    out = jnp.einsum("rkgl,rkld->rkgd", weight_cached, v_cache, preferred_element_type=F32)
    out = out + weight_fresh.astype(F32)[..., None] * fresh_value
    return out.reshape(rows, group * heads_kv * width).astype(BF16)


def expert_kernel(
    place, state, gate_w, up_w, router_w, ids, act, gate_sum, up_sum, route_sum, squares
):
    step = pl.program_id(0)
    width = state.shape[-1]
    gate = up = route = square = 0.0
    for block in range(state.shape[1]):
        hidden = state[:, block].reshape(-1, width)
        gate += jnp.dot(
            hidden, gate_w[:, block].reshape(width, -1), preferred_element_type=F32
        )
        up += jnp.dot(hidden, up_w[:, block].reshape(width, -1), preferred_element_type=F32)
        route += lax.dot_general(
            hidden, router_w[block], (((1,), (1,)), ((), ())), preferred_element_type=F32
        )
        wide = hidden.astype(F32)
        for start in range(0, width, 128):
            piece = wide[:, start : start + 128]
            square += piece * piece

    @pl.when(step == 0)
    def _():
        gate_sum[...] = gate
        up_sum[...] = up
        route_sum[...] = route
        squares[...] = square

    @pl.when(step > 0)
    def _():
        gate_sum[...] += gate
        up_sum[...] += up
        route_sum[...] += route
        squares[...] += square

    @pl.when(step == pl.num_programs(0) - 1)
    def _():
        expert = place[0]
        mean = jnp.sum(squares[...], axis=1, keepdims=True) / (width * NZ)
        scale = lax.rsqrt(mean + EPS)
        logits = route_sum[...] * scale
        lanes = lax.broadcasted_iota(jnp.int32, logits.shape, 1)
        first = ids[:, 0:1]
        second = ids[:, 1:2]
        first_logit = jnp.sum(jnp.where(lanes == first, logits, 0.0), axis=1, keepdims=True)
        second_logit = jnp.sum(jnp.where(lanes == second, logits, 0.0), axis=1, keepdims=True)
        is_first = first == expert
        gap = second_logit - first_logit
        weight = 1.0 / (1.0 + jnp.exp(jnp.where(is_first, gap, -gap)))
        weight = jnp.where(is_first | (second == expert), weight, 0.0)
        gated = gate_sum[...] * scale
        value = jax.nn.silu(gated) * (up_sum[...] * scale)
        act[...] = (weight * value).astype(BF16)


def experts(place, state, gate_w, up_w, router_w, ids):
    _, _, rows, width = state.shape
    total = NXY * rows
    hidden_units = gate_w.shape[-1]
    unit = width // NX
    step = 4
    weights = pl.BlockSpec((NX, step, unit, hidden_units), lambda z, p: (0, z, 0, 0))
    count = router_w.shape[1]
    return pl.pallas_call(
        expert_kernel,
        out_shape=jax.ShapeDtypeStruct((total, hidden_units), BF16),
        grid_spec=pltpu.PrefetchScalarGridSpec(
            num_scalar_prefetch=1,
            grid=(NZ // step,),
            in_specs=[
                pl.BlockSpec((NXY, step, rows, width), lambda z, p: (0, z, 0, 0)),
                weights,
                weights,
                pl.BlockSpec((step, count, width), lambda z, p: (z, 0, 0)),
                pl.BlockSpec((total, 2), lambda z, p: (0, 0)),
            ],
            out_specs=pl.BlockSpec((total, hidden_units), lambda z, p: (0, 0)),
            scratch_shapes=[
                pltpu.VMEM((total, hidden_units), F32),
                pltpu.VMEM((total, hidden_units), F32),
                pltpu.VMEM((total, count), F32),
                pltpu.VMEM((total, 128), F32),
            ],
        ),
        compiler_params=pltpu.CompilerParams(
            dimension_semantics=("arbitrary",), vmem_limit_bytes=32 << 20
        ),
        cost_estimate=pl.CostEstimate(
            flops=2 * total * width * NZ * 2 * hidden_units,
            bytes_accessed=10 << 20,
            transcendentals=total * hidden_units,
        ),
        name="experts",
    )(
        place,
        state,
        gate_w.reshape(NX, NZ, unit, hidden_units),
        up_w.reshape(NX, NZ, unit, hidden_units),
        router_w,
        ids,
    )


def down_kernel(
    place, mine_own, mine_other, theirs_own, theirs_other, w_mine, w_theirs, out
):
    width = out.shape[-1]
    core = place[1]
    for mine, theirs, which in (
        (mine_own, theirs_own, core),
        (mine_other, theirs_other, 1 - core),
    ):
        total = jnp.dot(mine[...], w_mine[...], preferred_element_type=F32)
        total += jnp.dot(theirs[...], w_theirs[...], preferred_element_type=F32)
        out[0, :, pl.ds(which, 1), :, :] = total.astype(BF16).reshape(NXY, 1, -1, width)


def down(place, acts, w_mine, w_theirs):
    total, units = acts[0].shape
    rows = total // NXY
    width = w_theirs.shape[1] // NX
    steps = 2
    block = width // steps
    return pl.pallas_call(
        down_kernel,
        out_shape=pltpu.HBM((NX, NXY, NC, rows, width), BF16),
        grid_spec=pltpu.PrefetchScalarGridSpec(
            num_scalar_prefetch=1,
            grid=(NX, steps),
            in_specs=[pl.BlockSpec((total, units), lambda x, s, p: (0, 0))] * 4
            + [
                pl.BlockSpec((units, block), lambda x, s, p: (0, (p[1] * NX + x) * steps + s)),
                pl.BlockSpec((units, block), lambda x, s, p: (0, x * steps + s)),
            ],
            out_specs=pl.BlockSpec(
                (1, NXY, NC, rows, block), lambda x, s, p: (x, 0, 0, 0, s)
            ),
        ),
        compiler_params=pltpu.CompilerParams(
            dimension_semantics=("arbitrary", "arbitrary"), vmem_limit_bytes=32 << 20
        ),
        cost_estimate=pl.CostEstimate(
            flops=8 * total * units * width * NX, bytes_accessed=7 << 20, transcendentals=0
        ),
        name="down",
    )(place, *acts, w_mine, w_theirs)


def head_kernel(own, other, w_own, w_other, below, out):
    width = own.shape[-1]
    vocab = w_own.shape[1]
    near = own[...].reshape(-1, width)
    far = other[...].reshape(-1, width)
    logits = jnp.dot(near, w_own[...], preferred_element_type=F32)
    logits += jnp.dot(far, w_other[...], preferred_element_type=F32)
    square = jnp.zeros((near.shape[0], 128), F32)
    for part in (near.astype(F32), far.astype(F32)):
        for start in range(0, width, 128):
            piece = part[:, start : start + 128]
            square += piece * piece
    square = jnp.sum(square, axis=1, keepdims=True)
    high = square.astype(BF16).astype(F32)
    lanes = lax.broadcasted_iota(jnp.int32, (near.shape[0], 128), 1)
    extra = jnp.where(lanes == 0, high, jnp.where(lanes == 1, square - high, 0.0))
    count = near.shape[0] // NX
    out[:, :count, :vocab] = logits.astype(BF16).reshape(NX, count, vocab)
    out[:, :count, vocab:] = extra.astype(BF16).reshape(NX, count, 128)
    out[:, count:, :] = below[...]


def head(own, other, w_own, w_other, below):
    vocab = w_own.shape[1]
    total = own.shape[0] * own.shape[1] * own.shape[2]
    rows = total // NX + below.shape[1]
    return pl.pallas_call(
        head_kernel,
        out_shape=pltpu.HBM((NX, rows, vocab + 128), BF16),
        compiler_params=pltpu.CompilerParams(vmem_limit_bytes=32 << 20),
        cost_estimate=pl.CostEstimate(
            flops=4 * total * own.shape[3] * vocab, bytes_accessed=4 << 20, transcendentals=0
        ),
        name="head",
    )(own, other, w_own, w_other, below)


def finish_kernel(place, parts, token, stats):
    count = token.shape[0]
    vocab = parts.shape[2] - 128
    total = jnp.sum(parts[:, :count, :].astype(F32), axis=0)
    square = jnp.sum(total[:, vocab:], axis=1, keepdims=True)
    logits = total[:, :vocab] * lax.rsqrt(square / place[1] + EPS)
    top = jnp.max(logits, axis=1, keepdims=True)
    summed = jnp.sum(jnp.exp(logits - top), axis=1, keepdims=True)
    slice_width = vocab // NX
    local = token[...] - place[0] * slice_width
    block = NZ * NY * NC * slice_width
    lanes = lax.broadcasted_iota(jnp.int32, logits.shape, 1)
    entry = (lanes // slice_width) * block + lanes % slice_width
    chosen = jnp.sum(jnp.where(entry == local, logits, 0.0), axis=1, keepdims=True)
    lane = lax.broadcasted_iota(jnp.int32, stats.shape, 1)
    stats[...] = jnp.where(lane == 0, top, jnp.where(lane == 1, summed, chosen))


def finish(place, parts, token):
    return pl.pallas_call(
        finish_kernel,
        out_shape=jax.ShapeDtypeStruct((token.shape[0], 128), F32),
        in_specs=[
            pl.BlockSpec(memory_space=pltpu.SMEM),
            pl.BlockSpec(memory_space=pltpu.VMEM),
            pl.BlockSpec(memory_space=pltpu.VMEM),
        ],
        compiler_params=pltpu.CompilerParams(vmem_limit_bytes=32 << 20),
        name="finish",
    )(place, parts, token)


def shards(
    queries,
    new_keys,
    new_values,
    k_cache,
    v_cache,
    lengths,
    residual,
    w_out,
    router,
    gain_moe,
    w_gate,
    w_up,
    w_down,
    expert_ids,
    gain_final,
    w_vocab,
    tokens,
    mu,
):
    x, z, y, core = (lax.axis_index(name) for name in ("x", "z", "y", "c"))
    expert = y * NC + core
    place = jnp.stack([expert, core]).astype(jnp.int32)
    width_all = gain_moe.shape[0]
    unit = w_out.shape[1]
    total_rows = residual.shape[0]
    part_rows = total_rows // (NX * NY * NC)

    packs = []
    for shift in range(NX):
        target = (x + shift) % NX
        rows = lax.dynamic_slice_in_dim(
            residual, (target * NY * NC + expert) * part_rows, part_rows
        )
        pack = jnp.concatenate([w_out, rows], axis=0)
        if shift:
            pack = lax.ppermute(pack, "x", [(i, (i + shift) % NX) for i in range(NX)])
        packs.append(pack)
    depth = w_out.shape[0]
    w_wide = jnp.concatenate([pack[:depth] for pack in packs], axis=1)
    residual_wide = jnp.concatenate([pack[depth:] for pack in packs], axis=1)

    half = width_all // NC
    slab = half // NX
    vocab_rows = w_vocab.reshape(NC, NX, slab, -1)
    vocab_parts = []
    for shift in range(NX):
        part = lax.dynamic_index_in_dim(vocab_rows, (x + shift) % NX, 1, keepdims=False)
        if shift:
            part = lax.ppermute(part, "x", [(i, (i + shift) % NX) for i in range(NX)])
        vocab_parts.append(part)
    gain_slab = gain_final.reshape(NC, NX, slab)
    gain_slab = lax.dynamic_index_in_dim(gain_slab, x, 1, keepdims=False)[:, :, None]
    columns = []
    for i in range(NX):
        away = (x - i) % NX
        part = vocab_parts[NX - 1]
        for shift in range(NX - 1):
            part = jnp.where(away == shift, vocab_parts[shift], part)
        columns.append((part.astype(F32) * gain_slab).astype(BF16))
    head_w = jnp.concatenate(columns, axis=2)
    head_own = lax.dynamic_index_in_dim(head_w, core, 0, keepdims=False)
    head_other = lax.dynamic_index_in_dim(head_w, 1 - core, 0, keepdims=False)

    down_sent = lax.dynamic_slice_in_dim(w_down[0], (1 - core) * half, half, axis=1)
    down_other = swap_cores(down_sent)

    attended = attend(queries, new_keys, new_values, k_cache, v_cache, lengths)
    attended_x = spread(attended, "z", NZ).reshape(-1, depth)
    partial_heads = jnp.dot(attended_x, w_wide, preferred_element_type=F32).astype(BF16)
    pieces = exchange(partial_heads.reshape(NY * NC, part_rows, NX * unit), EX)
    summed = jnp.sum(pieces.astype(F32), axis=0) + residual_wide.astype(F32)
    turned = summed.astype(BF16).reshape(part_rows, NX, unit)
    hidden = jnp.concatenate(
        [lax.dynamic_index_in_dim(turned, (x - i) % NX, 1, keepdims=False) for i in range(NX)],
        axis=1,
    )

    hidden_z = spread(hidden, "z", NZ)
    order = expert_ids.reshape(NXY, NC, part_rows, 2).transpose(1, 0, 2, 3)
    order = order.reshape(NC, -1, 2)
    order_own = lax.dynamic_index_in_dim(order, core, 0, keepdims=False)
    order_other = lax.dynamic_index_in_dim(order, 1 - core, 0, keepdims=False)
    gain_col = gain_moe[:, None]
    router_g = (router.astype(F32) * gain_col).astype(BF16)
    router_z = router_g.T.reshape(-1, NX, NZ, unit).transpose(2, 0, 1, 3)
    router_z = router_z.reshape(NZ, -1, NX * unit)
    gate_g = (w_gate[0].astype(F32) * gain_col).astype(BF16)
    up_g = (w_up[0].astype(F32) * gain_col).astype(BF16)
    ready = (hidden_z, gate_g, up_g, router_z, order_own, order_other)
    ready = lax.optimization_barrier(ready + (head_own, head_other, down_other))
    hidden_z, gate_g, up_g, router_z, order_own, order_other = ready[:6]
    head_own, head_other, down_other = ready[6:]
    own = spread(hidden_z, XY, NXY)
    other = swap_cores(own)

    act_own = experts(place, own, gate_g, up_g, router_z, order_own)
    act_other = experts(place, other, gate_g, up_g, router_z, order_other)
    acts = (act_own, act_other, swap_cores(act_other), swap_cores(act_own))
    sent = down(place, acts, w_down[0], down_other)
    sent = sent.reshape(NXY, NZ, part_rows, slab)
    sums = jnp.sum(exchange(sent, XY).astype(F32), axis=0).astype(BF16)
    sums = jnp.sum(exchange(sums, "z").astype(F32), axis=0)

    units = slab // unit
    first_unit = core * (half // unit) + x * units
    start = (y * NX + z // 2, first_unit % NZ, 0, 0)
    size = (1, units, part_rows, NX * unit)
    rows_here = jnp.where(
        z % 2 == core, lax.dynamic_slice(own, start, size), lax.dynamic_slice(other, start, size)
    )[0].reshape(units, part_rows, NX, unit)
    cut = lax.dynamic_index_in_dim(rows_here, first_unit // NZ, 2, keepdims=False)
    hidden_here = cut.transpose(1, 0, 2).reshape(part_rows, slab).astype(F32)
    moved = (hidden_here + sums).astype(BF16)

    final_own = spread(spread(moved, "z", NZ), "y", NY).reshape(NY, NZ, part_rows, slab)
    final_other = swap_cores(final_own)
    count = total_rows // NX

    own_rows = total_rows // (NX * NZ * NY * NC)
    size = (NX, 1, own_rows, slab)
    start = (0, z, expert * own_rows, 0)
    near = lax.dynamic_slice(final_own, start, size)
    far = lax.dynamic_slice(final_other, start, size)
    low = jnp.where(core == 0, near, far)
    high = jnp.where(core == 0, far, near)
    vocab = head_own.shape[1]
    rows_out = jnp.concatenate([low, high], axis=1).reshape(NX, -1, vocab)
    below = jnp.pad(rows_out, ((0, 0), (0, 16 - rows_out.shape[1]), (0, 128)))
    partial = head(final_own, final_other, head_own, head_other, below)
    parts = exchange(partial, "x")
    hidden_out = parts[:, count : count + rows_out.shape[1], :vocab]
    hidden_out = hidden_out.reshape(NX, NC, own_rows, slab).transpose(2, 1, 0, 3)
    hidden_out = hidden_out.reshape(own_rows, width_all)

    token = lax.dynamic_slice_in_dim(tokens, x * count, count)[:, None]
    where = jnp.stack([z * (NY * NC) + expert, jnp.int32(width_all)]).astype(jnp.int32)
    stats = finish(where, parts, token)
    flat = stats[:, :4].reshape(-1, own_rows * 4)
    flat = jnp.pad(flat, ((0, 0), (0, 128 - own_rows * 4)))
    got = exchange(flat, ("z", "y", "c"))[:, : own_rows * 4].reshape(-1, own_rows, 4)
    top = jnp.max(got[:, :, 0], axis=0)
    summed_all = jnp.sum(got[:, :, 1] * jnp.exp(got[:, :, 0] - top[None]), axis=0)
    chosen = jnp.sum(got[:, :, 2], axis=0)
    surprise = (top + jnp.log(summed_all) - chosen) / LOG_TWO
    mu_next = mu - RATE * (surprise - TARGET)
    return (hidden_out, surprise, mu_next)


def solution(mesh):
    fine = Mesh(mesh.devices.reshape(NX, NZ, NY, NC), ALL)
    dp = ("x", "z")
    return jax.shard_map(
        shards,
        mesh=fine,
        in_specs=(
            P(dp, EX),
            P(dp, EX),
            P(dp, EX),
            P(dp, EX, None, None),
            P(dp, EX, None, None),
            P(dp),
            P(None, dp),
            P(EX, dp),
            P(),
            P(),
            P(EX, None, dp),
            P(EX, None, dp),
            P(EX, dp, None),
            P(),
            P(),
            P(None, ALL),
            P(),
            P(ALL),
        ),
        out_specs=(P(ALL, None), P(ALL), P(ALL)),
        check_vma=False,
    )
```

```python
import jax
import jax.numpy as jnp
from jax import lax
from jax.experimental import pallas as pl
from jax.experimental.pallas import tpu as pltpu
from jax.sharding import Mesh
from jax.sharding import PartitionSpec as P

EPS = 1e-05
TARGET = 5.0
RATE = 0.1
LOG_TWO = 0.6931471805599453
F32 = jnp.float32
BF16 = jnp.bfloat16
NX, NZ, NY, NC = 4, 8, 4, 2
NXY = NX * NY
XY = ("x", "y")
EX = ("y", "c")
ALL = ("x", "z", "y", "c")


def swap_cores(value):
    return lax.ppermute(value, "c", [(0, 1), (1, 0)])


def exchange(value, axes):
    return lax.all_to_all(value, axes, split_axis=0, concat_axis=0, tiled=True)


def spread(value, axes, count):
    return exchange(jnp.broadcast_to(value[None], (count,) + value.shape), axes)


def attend(queries, new_keys, new_values, k_cache, v_cache, lengths):
    rows, heads_kv, span, width = k_cache.shape
    group = queries.shape[1] // (heads_kv * width)
    query = queries.reshape(rows, heads_kv, group, width)
    scale = width ** (-0.5)
    cached = (
        jnp.einsum("rkgd,rkld->rkgl", query, k_cache, preferred_element_type=F32) * scale
    )
    fresh_key = new_keys.reshape(rows, heads_kv, width)
    fresh = jnp.einsum("rkgd,rkd->rkg", query, fresh_key, preferred_element_type=F32) * scale
    live = jnp.arange(span, dtype=jnp.int32)[None, :] < lengths[:, None]
    cached = jnp.where(live[:, None, None, :], cached, -1e30)
    top = jnp.maximum(jnp.max(cached, axis=-1), fresh)
    part_cached = jnp.exp(cached - top[..., None])
    part_fresh = jnp.exp(fresh - top)
    total = jnp.sum(part_cached, axis=-1) + part_fresh
    weight_cached = (part_cached / total[..., None]).astype(BF16)
    weight_fresh = (part_fresh / total).astype(BF16)
    fresh_value = new_values.reshape(rows, heads_kv, 1, width).astype(F32)
    out = jnp.einsum("rkgl,rkld->rkgd", weight_cached, v_cache, preferred_element_type=F32)
    out = out + weight_fresh.astype(F32)[..., None] * fresh_value
    return out.reshape(rows, group * heads_kv * width).astype(BF16)


def project_kernel(place, attended, *refs):
    packs, (partial, residual) = refs[:NX], refs[NX:]
    depth = attended.shape[-1]
    value = attended[...].reshape(-1, depth)
    products = [
        jnp.dot(value, pack[:depth, :], preferred_element_type=F32) for pack in packs
    ]
    rows = [pack[depth:, :].astype(F32) for pack in packs]
    x = place[2]

    def order(parts):
        blocks = []
        for i in range(NX):
            away = lax.rem(x - i + NX, NX)
            block = parts[NX - 1]
            for shift in range(NX - 1):
                block = jnp.where(away == shift, parts[shift], block)
            blocks.append(block)
        return jnp.concatenate(blocks, axis=1).astype(BF16)

    partial[...] = order(products).reshape(partial.shape)
    residual[...] = order(rows)


def project(place, attended, packs):
    depth, unit = attended.shape[-1], packs[0].shape[1]
    rows = packs[0].shape[0] - depth
    vmem = pl.BlockSpec(memory_space=pltpu.VMEM)
    return pl.pallas_call(
        project_kernel,
        out_shape=(
            jax.ShapeDtypeStruct((NY * NC, rows, NX * unit), BF16),
            jax.ShapeDtypeStruct((rows, NX * unit), BF16),
        ),
        in_specs=[pl.BlockSpec(memory_space=pltpu.SMEM)] + [vmem] * (1 + NX),
        out_specs=(vmem, vmem),
        compiler_params=pltpu.CompilerParams(vmem_limit_bytes=32 << 20),
        cost_estimate=pl.CostEstimate(
            flops=2 * NZ * rows * depth * NX * unit, bytes_accessed=2 << 20, transcendentals=0
        ),
        name="project",
    )(place, attended, *packs)


def expert_kernel(
    place, state, gate_w, up_w, router_w, ids, act, gate_sum, up_sum, route_sum, squares
):
    step = pl.program_id(0)
    width = state.shape[-1]
    gate = up = route = square = 0.0
    for block in range(state.shape[1]):
        hidden = state[:, block].reshape(-1, width)
        gate += jnp.dot(
            hidden, gate_w[:, block].reshape(width, -1), preferred_element_type=F32
        )
        up += jnp.dot(hidden, up_w[:, block].reshape(width, -1), preferred_element_type=F32)
        route += lax.dot_general(
            hidden, router_w[block], (((1,), (1,)), ((), ())), preferred_element_type=F32
        )
        wide = hidden.astype(F32)
        for start in range(0, width, 128):
            piece = wide[:, start : start + 128]
            square += piece * piece

    @pl.when(step == 0)
    def _():
        gate_sum[...] = gate
        up_sum[...] = up
        route_sum[...] = route
        squares[...] = square

    @pl.when(step > 0)
    def _():
        gate_sum[...] += gate
        up_sum[...] += up
        route_sum[...] += route
        squares[...] += square

    @pl.when(step == pl.num_programs(0) - 1)
    def _():
        expert = place[0]
        mean = jnp.sum(squares[...], axis=1, keepdims=True) / (width * NZ)
        scale = lax.rsqrt(mean + EPS)
        logits = route_sum[...] * scale
        lanes = lax.broadcasted_iota(jnp.int32, logits.shape, 1)
        first = ids[:, 0:1]
        second = ids[:, 1:2]
        first_logit = jnp.sum(jnp.where(lanes == first, logits, 0.0), axis=1, keepdims=True)
        second_logit = jnp.sum(jnp.where(lanes == second, logits, 0.0), axis=1, keepdims=True)
        is_first = first == expert
        gap = second_logit - first_logit
        weight = 1.0 / (1.0 + jnp.exp(jnp.where(is_first, gap, -gap)))
        weight = jnp.where(is_first | (second == expert), weight, 0.0)
        gated = gate_sum[...] * scale
        value = jax.nn.silu(gated) * (up_sum[...] * scale)
        act[...] = (weight * value).astype(BF16)


def experts(place, state, gate_w, up_w, router_w, ids):
    _, _, rows, width = state.shape
    total = NXY * rows
    hidden_units = gate_w.shape[-1]
    unit = width // NX
    step = 4
    weights = pl.BlockSpec((NX, step, unit, hidden_units), lambda z, p: (0, z, 0, 0))
    count = router_w.shape[1]
    return pl.pallas_call(
        expert_kernel,
        out_shape=jax.ShapeDtypeStruct((total, hidden_units), BF16),
        grid_spec=pltpu.PrefetchScalarGridSpec(
            num_scalar_prefetch=1,
            grid=(NZ // step,),
            in_specs=[
                pl.BlockSpec((NXY, step, rows, width), lambda z, p: (0, z, 0, 0)),
                weights,
                weights,
                pl.BlockSpec((step, count, width), lambda z, p: (z, 0, 0)),
                pl.BlockSpec((total, 2), lambda z, p: (0, 0)),
            ],
            out_specs=pl.BlockSpec((total, hidden_units), lambda z, p: (0, 0)),
            scratch_shapes=[
                pltpu.VMEM((total, hidden_units), F32),
                pltpu.VMEM((total, hidden_units), F32),
                pltpu.VMEM((total, count), F32),
                pltpu.VMEM((total, 128), F32),
            ],
        ),
        compiler_params=pltpu.CompilerParams(
            dimension_semantics=("arbitrary",), vmem_limit_bytes=32 << 20
        ),
        cost_estimate=pl.CostEstimate(
            flops=2 * total * width * NZ * 2 * hidden_units,
            bytes_accessed=10 << 20,
            transcendentals=total * hidden_units,
        ),
        name="experts",
    )(
        place,
        state,
        gate_w.reshape(NX, NZ, unit, hidden_units),
        up_w.reshape(NX, NZ, unit, hidden_units),
        router_w,
        ids,
    )


def down_kernel(
    place, mine_own, mine_other, theirs_own, theirs_other, w_mine, w_theirs, out
):
    width = out.shape[-1]
    core = place[1]
    for mine, theirs, which in (
        (mine_own, theirs_own, core),
        (mine_other, theirs_other, 1 - core),
    ):
        total = jnp.dot(mine[...], w_mine[...], preferred_element_type=F32)
        total += jnp.dot(theirs[...], w_theirs[...], preferred_element_type=F32)
        out[0, :, pl.ds(which, 1), :, :] = total.astype(BF16).reshape(NXY, 1, -1, width)


def down(place, acts, w_mine, w_theirs):
    total, units = acts[0].shape
    rows = total // NXY
    width = w_theirs.shape[1] // NX
    return pl.pallas_call(
        down_kernel,
        out_shape=pltpu.HBM((NX, NXY, NC, rows, width), BF16),
        grid_spec=pltpu.PrefetchScalarGridSpec(
            num_scalar_prefetch=1,
            grid=(NX,),
            in_specs=[pl.BlockSpec((total, units), lambda x, p: (0, 0))] * 4
            + [
                pl.BlockSpec((units, width), lambda x, p: (0, p[1] * NX + x)),
                pl.BlockSpec((units, width), lambda x, p: (0, x)),
            ],
            out_specs=pl.BlockSpec((1, NXY, NC, rows, width), lambda x, p: (x, 0, 0, 0, 0)),
        ),
        compiler_params=pltpu.CompilerParams(
            dimension_semantics=("arbitrary",), vmem_limit_bytes=32 << 20
        ),
        cost_estimate=pl.CostEstimate(
            flops=8 * total * units * width * NX, bytes_accessed=7 << 20, transcendentals=0
        ),
        name="down",
    )(place, *acts, w_mine, w_theirs)


def head_kernel(own, other, w_own, w_other, below, out):
    width = own.shape[-1]
    vocab = w_own.shape[1]
    near = own[...].reshape(-1, width)
    far = other[...].reshape(-1, width)
    logits = jnp.dot(near, w_own[...], preferred_element_type=F32)
    logits += jnp.dot(far, w_other[...], preferred_element_type=F32)
    square = jnp.zeros((near.shape[0], 128), F32)
    for part in (near.astype(F32), far.astype(F32)):
        for start in range(0, width, 128):
            piece = part[:, start : start + 128]
            square += piece * piece
    square = jnp.sum(square, axis=1, keepdims=True)
    high = square.astype(BF16).astype(F32)
    lanes = lax.broadcasted_iota(jnp.int32, (near.shape[0], 128), 1)
    extra = jnp.where(lanes == 0, high, jnp.where(lanes == 1, square - high, 0.0))
    count = near.shape[0] // NX
    out[:, :count, :vocab] = logits.astype(BF16).reshape(NX, count, vocab)
    out[:, :count, vocab:] = extra.astype(BF16).reshape(NX, count, 128)
    out[:, count:, :] = below[...]


def head(own, other, w_own, w_other, below):
    vocab = w_own.shape[1]
    total = own.shape[0] * own.shape[1] * own.shape[2]
    rows = total // NX + below.shape[1]
    return pl.pallas_call(
        head_kernel,
        out_shape=pltpu.HBM((NX, rows, vocab + 128), BF16),
        compiler_params=pltpu.CompilerParams(vmem_limit_bytes=32 << 20),
        cost_estimate=pl.CostEstimate(
            flops=4 * total * own.shape[3] * vocab, bytes_accessed=4 << 20, transcendentals=0
        ),
        name="head",
    )(own, other, w_own, w_other, below)


def finish_kernel(place, parts, token, stats):
    count = token.shape[0]
    vocab = parts.shape[2] - 128
    total = jnp.sum(parts[:, :count, :].astype(F32), axis=0)
    square = jnp.sum(total[:, vocab:], axis=1, keepdims=True)
    logits = total[:, :vocab] * lax.rsqrt(square / place[1] + EPS)
    top = jnp.max(logits, axis=1, keepdims=True)
    summed = jnp.sum(jnp.exp(logits - top), axis=1, keepdims=True)
    slice_width = vocab // NX
    local = token[...] - place[0] * slice_width
    block = NZ * NY * NC * slice_width
    lanes = lax.broadcasted_iota(jnp.int32, logits.shape, 1)
    entry = (lanes // slice_width) * block + lanes % slice_width
    chosen = jnp.sum(jnp.where(entry == local, logits, 0.0), axis=1, keepdims=True)
    lane = lax.broadcasted_iota(jnp.int32, stats.shape, 1)
    stats[...] = jnp.where(lane == 0, top, jnp.where(lane == 1, summed, chosen))


def finish(place, parts, token):
    return pl.pallas_call(
        finish_kernel,
        out_shape=jax.ShapeDtypeStruct((token.shape[0], 128), F32),
        in_specs=[
            pl.BlockSpec(memory_space=pltpu.SMEM),
            pl.BlockSpec(memory_space=pltpu.VMEM),
            pl.BlockSpec(memory_space=pltpu.VMEM),
        ],
        compiler_params=pltpu.CompilerParams(vmem_limit_bytes=32 << 20),
        name="finish",
    )(place, parts, token)


def shards(
    queries,
    new_keys,
    new_values,
    k_cache,
    v_cache,
    lengths,
    residual,
    w_out,
    router,
    gain_moe,
    w_gate,
    w_up,
    w_down,
    expert_ids,
    gain_final,
    w_vocab,
    tokens,
    mu,
):
    x, z, y, core = (lax.axis_index(name) for name in ("x", "z", "y", "c"))
    expert = y * NC + core
    place = jnp.stack([expert, core, x]).astype(jnp.int32)
    width_all = gain_moe.shape[0]
    unit = w_out.shape[1]
    total_rows = residual.shape[0]
    part_rows = total_rows // (NX * NY * NC)

    sends = []
    for shift in range(NX):
        target = (x + shift) % NX
        rows = lax.dynamic_slice_in_dim(
            residual, (target * NY * NC + expert) * part_rows, part_rows
        )
        sends.append(jnp.concatenate([w_out, rows], axis=0))
    packs = [sends[0]]
    for shift in range(1, NX):
        pairs = [(i, (i + shift) % NX) for i in range(NX)]
        packs.append(lax.ppermute(sends[shift], "x", pairs))
    depth = w_out.shape[0]

    attended = attend(queries, new_keys, new_values, k_cache, v_cache, lengths)
    attended_x = spread(attended, "z", NZ)
    partial_heads, residual_here = project(place, attended_x, packs)
    late = (partial_heads, expert_ids, w_vocab, w_gate, w_up, w_down, router)
    late = lax.optimization_barrier(late)
    partial_heads, expert_ids, w_vocab, w_gate, w_up, w_down, router = late
    half = width_all // NC
    slab = half // NX
    vocab_rows = w_vocab.reshape(NC, NX, slab, -1)
    vocab_parts = []
    for shift in range(NX):
        part = lax.dynamic_index_in_dim(vocab_rows, (x + shift) % NX, 1, keepdims=False)
        if shift:
            part = lax.ppermute(part, "x", [(i, (i + shift) % NX) for i in range(NX)])
        vocab_parts.append(part)
    gain_slab = gain_final.reshape(NC, NX, slab)
    gain_slab = lax.dynamic_index_in_dim(gain_slab, x, 1, keepdims=False)[:, :, None]
    columns = []
    for i in range(NX):
        away = (x - i) % NX
        part = vocab_parts[NX - 1]
        for shift in range(NX - 1):
            part = jnp.where(away == shift, vocab_parts[shift], part)
        columns.append((part.astype(F32) * gain_slab).astype(BF16))
    head_w = jnp.concatenate(columns, axis=2)
    head_own = lax.dynamic_index_in_dim(head_w, core, 0, keepdims=False)
    head_other = lax.dynamic_index_in_dim(head_w, 1 - core, 0, keepdims=False)

    down_sent = lax.dynamic_slice_in_dim(w_down[0], (1 - core) * half, half, axis=1)
    down_other = swap_cores(down_sent)

    pieces = exchange(partial_heads, EX)
    hidden = jnp.sum(pieces.astype(F32), axis=0) + residual_here.astype(F32)
    hidden = hidden.astype(BF16)

    hidden_z = spread(hidden, "z", NZ)
    order = expert_ids.reshape(NXY, NC, part_rows, 2).transpose(1, 0, 2, 3)
    order = order.reshape(NC, -1, 2)
    order_own = lax.dynamic_index_in_dim(order, core, 0, keepdims=False)
    order_other = lax.dynamic_index_in_dim(order, 1 - core, 0, keepdims=False)
    gain_col = gain_moe[:, None]
    router_g = (router.astype(F32) * gain_col).astype(BF16)
    router_z = router_g.T.reshape(-1, NX, NZ, unit).transpose(2, 0, 1, 3)
    router_z = router_z.reshape(NZ, -1, NX * unit)
    gate_g = (w_gate[0].astype(F32) * gain_col).astype(BF16)
    up_g = (w_up[0].astype(F32) * gain_col).astype(BF16)
    ready = (hidden_z, gate_g, up_g, router_z, order_own, order_other)
    ready = lax.optimization_barrier(ready + (head_own, head_other, down_other))
    hidden_z, gate_g, up_g, router_z, order_own, order_other = ready[:6]
    head_own, head_other, down_other = ready[6:]
    own = spread(hidden_z, XY, NXY)
    other = swap_cores(own)

    act_own = experts(place, own, gate_g, up_g, router_z, order_own)
    act_other = experts(place, other, gate_g, up_g, router_z, order_other)
    acts = (act_own, act_other, swap_cores(act_other), swap_cores(act_own))
    sent = down(place, acts, w_down[0], down_other)
    sent = sent.reshape(NXY, NZ, part_rows, slab)
    sums = jnp.sum(exchange(sent, XY).astype(F32), axis=0).astype(BF16)
    sums = jnp.sum(exchange(sums, "z").astype(F32), axis=0)

    units = slab // unit
    first_unit = core * (half // unit) + x * units
    start = (y * NX + z // 2, first_unit % NZ, 0, 0)
    size = (1, units, part_rows, NX * unit)
    rows_here = jnp.where(
        z % 2 == core, lax.dynamic_slice(own, start, size), lax.dynamic_slice(other, start, size)
    )[0].reshape(units, part_rows, NX, unit)
    cut = lax.dynamic_index_in_dim(rows_here, first_unit // NZ, 2, keepdims=False)
    hidden_here = cut.transpose(1, 0, 2).reshape(part_rows, slab).astype(F32)
    moved = (hidden_here + sums).astype(BF16)

    final_own = spread(spread(moved, "z", NZ), "y", NY).reshape(NY, NZ, part_rows, slab)
    final_other = swap_cores(final_own)
    count = total_rows // NX

    own_rows = total_rows // (NX * NZ * NY * NC)
    size = (NX, 1, own_rows, slab)
    start = (0, z, expert * own_rows, 0)
    near = lax.dynamic_slice(final_own, start, size)
    far = lax.dynamic_slice(final_other, start, size)
    low = jnp.where(core == 0, near, far)
    high = jnp.where(core == 0, far, near)
    vocab = head_own.shape[1]
    rows_out = jnp.concatenate([low, high], axis=1).reshape(NX, -1, vocab)
    below = jnp.pad(rows_out, ((0, 0), (0, 16 - rows_out.shape[1]), (0, 128)))
    partial = head(final_own, final_other, head_own, head_other, below)
    parts = exchange(partial, "x")
    hidden_out = parts[:, count : count + rows_out.shape[1], :vocab]
    hidden_out = hidden_out.reshape(NX, NC, own_rows, slab).transpose(2, 1, 0, 3)
    hidden_out = hidden_out.reshape(own_rows, width_all)

    token = lax.dynamic_slice_in_dim(tokens, x * count, count)[:, None]
    where = jnp.stack([z * (NY * NC) + expert, jnp.int32(width_all)]).astype(jnp.int32)
    stats = finish(where, parts, token)
    flat = stats[:, :4].reshape(-1, own_rows * 4)
    flat = jnp.pad(flat, ((0, 0), (0, 128 - own_rows * 4)))
    got = exchange(flat, ("z", "y", "c"))[:, : own_rows * 4].reshape(-1, own_rows, 4)
    top = jnp.max(got[:, :, 0], axis=0)
    summed_all = jnp.sum(got[:, :, 1] * jnp.exp(got[:, :, 0] - top[None]), axis=0)
    chosen = jnp.sum(got[:, :, 2], axis=0)
    surprise = (top + jnp.log(summed_all) - chosen) / LOG_TWO
    mu_next = mu - RATE * (surprise - TARGET)
    return (hidden_out, surprise, mu_next)


def solution(mesh):
    fine = Mesh(mesh.devices.reshape(NX, NZ, NY, NC), ALL)
    dp = ("x", "z")
    return jax.shard_map(
        shards,
        mesh=fine,
        in_specs=(
            P(dp, EX),
            P(dp, EX),
            P(dp, EX),
            P(dp, EX, None, None),
            P(dp, EX, None, None),
            P(dp),
            P(None, dp),
            P(EX, dp),
            P(),
            P(),
            P(EX, None, dp),
            P(EX, None, dp),
            P(EX, dp, None),
            P(),
            P(),
            P(None, ALL),
            P(),
            P(ALL),
        ),
        out_specs=(P(ALL, None), P(ALL), P(ALL)),
        check_vma=False,
    )
```

```python
import jax
import jax.numpy as jnp
from jax import lax
from jax.experimental import pallas as pl
from jax.experimental.pallas import tpu as pltpu
from jax.sharding import Mesh
from jax.sharding import PartitionSpec as P

EPS = 1e-05
TARGET = 5.0
RATE = 0.1
LOG_TWO = 0.6931471805599453
F32 = jnp.float32
BF16 = jnp.bfloat16
NX, NZ, NY, NC = 4, 8, 4, 2
NXY = NX * NY
XY = ("x", "y")
EX = ("y", "c")
ALL = ("x", "z", "y", "c")


def swap_cores(value):
    return lax.ppermute(value, "c", [(0, 1), (1, 0)])


def exchange(value, axes):
    return lax.all_to_all(value, axes, split_axis=0, concat_axis=0, tiled=True)


def spread(value, axes, count):
    return exchange(jnp.broadcast_to(value[None], (count,) + value.shape), axes)


def attend_kernel(lengths, queries, new_keys, new_values, k_cache, v_cache, out):
    rows, _, span, width = k_cache.shape
    group = queries.shape[1] // width
    total = group * rows
    query = jnp.concatenate(
        [queries[:, h * width : (h + 1) * width] for h in range(group)], axis=0
    )
    scale = width ** (-0.5)
    keys = k_cache[...].reshape(rows * span, width)
    scores = (
        lax.dot_general(query, keys, (((1,), (1,)), ((), ())), preferred_element_type=F32) * scale
    )
    fresh_key = jnp.concatenate([new_keys[...].astype(F32)] * group, axis=0)
    fresh = jnp.sum(query.astype(F32) * fresh_key, axis=1, keepdims=True) * scale
    request = lax.broadcasted_iota(jnp.int32, (total, 1), 0) % rows
    first = request * span
    last = first
    for r in range(rows):
        last = jnp.where(request == r, r * span + lengths[r], last)
    column = lax.broadcasted_iota(jnp.int32, scores.shape, 1)
    scores = jnp.where((column >= first) & (column < last), scores, -1e30)
    top = jnp.maximum(jnp.max(scores, axis=1, keepdims=True), fresh)
    part = jnp.exp(scores - top)
    part_fresh = jnp.exp(fresh - top)
    sums = jnp.sum(part, axis=1, keepdims=True) + part_fresh
    weight = (part / sums).astype(BF16)
    weight_fresh = (part_fresh / sums).astype(BF16).astype(F32)
    values = v_cache[...].reshape(rows * span, width)
    result = jnp.dot(weight, values, preferred_element_type=F32)
    fresh_value = jnp.concatenate([new_values[...].astype(F32)] * group, axis=0)
    result = (result + weight_fresh * fresh_value).astype(BF16)
    wide = jnp.concatenate([result[h * rows : (h + 1) * rows] for h in range(group)], axis=1)
    for z in range(out.shape[0]):
        out[z] = wide


def attend(queries, new_keys, new_values, k_cache, v_cache, lengths):
    rows, width = queries.shape
    vmem = pl.BlockSpec(memory_space=pltpu.VMEM)
    return pl.pallas_call(
        attend_kernel,
        out_shape=pltpu.HBM((NZ, rows, width), BF16),
        in_specs=[pl.BlockSpec(memory_space=pltpu.SMEM)] + [vmem] * 5,
        out_specs=vmem,
        compiler_params=pltpu.CompilerParams(vmem_limit_bytes=32 << 20),
        cost_estimate=pl.CostEstimate(flops=2 << 34, bytes_accessed=2 << 20, transcendentals=0),
        name="attend",
    )(lengths, queries, new_keys, new_values, k_cache, v_cache)


def pack_kernel(place, w_out, residual, *packs):
    unit, depth = w_out.shape
    rows = packs[0].shape[0] - unit
    line = lax.broadcasted_iota(jnp.int32, (NX * rows, residual.shape[1]), 0)
    target = lax.rem(place[2] + line // rows, NX)
    wanted = (target * NY * NC + place[0]) * rows + line % rows
    pick = lax.broadcasted_iota(jnp.int32, line.shape, 1) == wanted
    parts = lax.dot_general(
        pick.astype(F32).astype(BF16),
        residual[...],
        (((1,), (1,)), ((), ())),
        preferred_element_type=F32,
    )
    for shift, pack in enumerate(packs):
        part = parts[shift * rows : (shift + 1) * rows, :]
        pack[:unit, :] = w_out[...]
        pack[unit:, :] = jnp.concatenate(
            [part, jnp.zeros((rows, depth - unit), F32)], axis=1
        ).astype(BF16)


def pack(place, w_out, residual, rows):
    unit, depth = w_out.shape
    shape = (unit + rows, depth)
    vmem = pl.BlockSpec(memory_space=pltpu.VMEM)
    return pl.pallas_call(
        pack_kernel,
        out_shape=[jax.ShapeDtypeStruct(shape, BF16)] + [pltpu.HBM(shape, BF16)] * (NX - 1),
        in_specs=[pl.BlockSpec(memory_space=pltpu.SMEM), vmem, vmem],
        out_specs=[vmem] * NX,
        compiler_params=pltpu.CompilerParams(vmem_limit_bytes=32 << 20),
        name="pack",
    )(place, w_out, residual)


def project_kernel(place, attended, *refs):
    packs, (partial, residual) = refs[:NX], refs[NX:]
    depth = attended.shape[-1]
    value = attended[...].reshape(-1, depth)
    unit = residual.shape[1] // NX
    products = [
        lax.dot_general(
            value, pack[:unit, :], (((1,), (1,)), ((), ())), preferred_element_type=F32
        )
        for pack in packs
    ]
    rows = [pack[unit:, :].astype(F32)[:, :unit] for pack in packs]
    x = place[2]

    def order(parts):
        blocks = []
        for i in range(NX):
            away = lax.rem(x - i + NX, NX)
            block = parts[NX - 1]
            for shift in range(NX - 1):
                block = jnp.where(away == shift, parts[shift], block)
            blocks.append(block)
        return jnp.concatenate(blocks, axis=1).astype(BF16)

    partial[...] = order(products).reshape(partial.shape)
    residual[...] = order(rows)


def project(place, attended, packs):
    _, rows, depth = attended.shape
    unit = packs[0].shape[0] - rows
    vmem = pl.BlockSpec(memory_space=pltpu.VMEM)
    return pl.pallas_call(
        project_kernel,
        out_shape=(
            jax.ShapeDtypeStruct((NY * NC, rows, NX * unit), BF16),
            jax.ShapeDtypeStruct((rows, NX * unit), BF16),
        ),
        in_specs=[pl.BlockSpec(memory_space=pltpu.SMEM)] + [vmem] * (1 + NX),
        out_specs=(vmem, vmem),
        compiler_params=pltpu.CompilerParams(vmem_limit_bytes=32 << 20),
        cost_estimate=pl.CostEstimate(
            flops=2 * NZ * rows * depth * NX * unit, bytes_accessed=2 << 20, transcendentals=0
        ),
        name="project",
    )(place, attended, *packs)


def expert_kernel(
    place, state, gate_w, up_w, router_w, ids, act, gate_sum, up_sum, route_sum, squares
):
    step = pl.program_id(0)
    width = state.shape[-1]
    gate = up = route = square = 0.0
    for block in range(state.shape[1]):
        hidden = state[:, block].reshape(-1, width)
        gate += jnp.dot(
            hidden, gate_w[:, block].reshape(width, -1), preferred_element_type=F32
        )
        up += jnp.dot(hidden, up_w[:, block].reshape(width, -1), preferred_element_type=F32)
        route += lax.dot_general(
            hidden, router_w[block], (((1,), (1,)), ((), ())), preferred_element_type=F32
        )
        wide = hidden.astype(F32)
        for start in range(0, width, 128):
            piece = wide[:, start : start + 128]
            square += piece * piece

    @pl.when(step == 0)
    def _():
        gate_sum[...] = gate
        up_sum[...] = up
        route_sum[...] = route
        squares[...] = square

    @pl.when(step > 0)
    def _():
        gate_sum[...] += gate
        up_sum[...] += up
        route_sum[...] += route
        squares[...] += square

    @pl.when(step == pl.num_programs(0) - 1)
    def _():
        expert = place[0]
        mean = jnp.sum(squares[...], axis=1, keepdims=True) / (width * NZ)
        scale = lax.rsqrt(mean + EPS)
        logits = route_sum[...] * scale
        lanes = lax.broadcasted_iota(jnp.int32, logits.shape, 1)
        first = ids[:, 0:1]
        second = ids[:, 1:2]
        first_logit = jnp.sum(jnp.where(lanes == first, logits, 0.0), axis=1, keepdims=True)
        second_logit = jnp.sum(jnp.where(lanes == second, logits, 0.0), axis=1, keepdims=True)
        is_first = first == expert
        gap = second_logit - first_logit
        weight = 1.0 / (1.0 + jnp.exp(jnp.where(is_first, gap, -gap)))
        weight = jnp.where(is_first | (second == expert), weight, 0.0)
        gated = gate_sum[...] * scale
        value = jax.nn.silu(gated) * (up_sum[...] * scale)
        act[...] = (weight * value).astype(BF16)


def experts(place, state, gate_w, up_w, router_w, ids):
    _, _, rows, width = state.shape
    total = NXY * rows
    hidden_units = gate_w.shape[-1]
    unit = width // NX
    step = 4
    weights = pl.BlockSpec((NX, step, unit, hidden_units), lambda z, p: (0, z, 0, 0))
    count = router_w.shape[1]
    return pl.pallas_call(
        expert_kernel,
        out_shape=jax.ShapeDtypeStruct((total, hidden_units), BF16),
        grid_spec=pltpu.PrefetchScalarGridSpec(
            num_scalar_prefetch=1,
            grid=(NZ // step,),
            in_specs=[
                pl.BlockSpec((NXY, step, rows, width), lambda z, p: (0, z, 0, 0)),
                weights,
                weights,
                pl.BlockSpec((step, count, width), lambda z, p: (z, 0, 0)),
                pl.BlockSpec((total, 2), lambda z, p: (0, 0)),
            ],
            out_specs=pl.BlockSpec((total, hidden_units), lambda z, p: (0, 0)),
            scratch_shapes=[
                pltpu.VMEM((total, hidden_units), F32),
                pltpu.VMEM((total, hidden_units), F32),
                pltpu.VMEM((total, count), F32),
                pltpu.VMEM((total, 128), F32),
            ],
        ),
        compiler_params=pltpu.CompilerParams(
            dimension_semantics=("arbitrary",), vmem_limit_bytes=32 << 20
        ),
        cost_estimate=pl.CostEstimate(
            flops=2 * total * width * NZ * 2 * hidden_units,
            bytes_accessed=10 << 20,
            transcendentals=total * hidden_units,
        ),
        name="experts",
    )(
        place,
        state,
        gate_w.reshape(NX, NZ, unit, hidden_units),
        up_w.reshape(NX, NZ, unit, hidden_units),
        router_w,
        ids,
    )


def down_kernel(
    place, mine_own, mine_other, theirs_own, theirs_other, w_mine, w_theirs, out
):
    width = out.shape[-1]
    core = place[1]
    for mine, theirs, which in (
        (mine_own, theirs_own, core),
        (mine_other, theirs_other, 1 - core),
    ):
        total = jnp.dot(mine[...], w_mine[...], preferred_element_type=F32)
        total += jnp.dot(theirs[...], w_theirs[...], preferred_element_type=F32)
        out[0, :, pl.ds(which, 1), :, :] = total.astype(BF16).reshape(NXY, 1, -1, width)


def down(place, acts, w_mine, w_theirs):
    total, units = acts[0].shape
    rows = total // NXY
    width = w_theirs.shape[1] // NX
    return pl.pallas_call(
        down_kernel,
        out_shape=pltpu.HBM((NX, NXY, NC, rows, width), BF16),
        grid_spec=pltpu.PrefetchScalarGridSpec(
            num_scalar_prefetch=1,
            grid=(NX,),
            in_specs=[pl.BlockSpec((total, units), lambda x, p: (0, 0))] * 4
            + [
                pl.BlockSpec((units, width), lambda x, p: (0, p[1] * NX + x)),
                pl.BlockSpec((units, width), lambda x, p: (0, x)),
            ],
            out_specs=pl.BlockSpec((1, NXY, NC, rows, width), lambda x, p: (x, 0, 0, 0, 0)),
        ),
        compiler_params=pltpu.CompilerParams(
            dimension_semantics=("arbitrary",), vmem_limit_bytes=32 << 20
        ),
        cost_estimate=pl.CostEstimate(
            flops=8 * total * units * width * NX, bytes_accessed=7 << 20, transcendentals=0
        ),
        name="down",
    )(place, *acts, w_mine, w_theirs)


def head_kernel(own, other, w_own, w_other, below, out):
    width = own.shape[-1]
    vocab = w_own.shape[1]
    near = own[...].reshape(-1, width)
    far = other[...].reshape(-1, width)
    logits = jnp.dot(near, w_own[...], preferred_element_type=F32)
    logits += jnp.dot(far, w_other[...], preferred_element_type=F32)
    square = jnp.zeros((near.shape[0], 128), F32)
    for part in (near.astype(F32), far.astype(F32)):
        for start in range(0, width, 128):
            piece = part[:, start : start + 128]
            square += piece * piece
    square = jnp.sum(square, axis=1, keepdims=True)
    high = square.astype(BF16).astype(F32)
    lanes = lax.broadcasted_iota(jnp.int32, (near.shape[0], 128), 1)
    extra = jnp.where(lanes == 0, high, jnp.where(lanes == 1, square - high, 0.0))
    count = near.shape[0] // NX
    out[:, :count, :vocab] = logits.astype(BF16).reshape(NX, count, vocab)
    out[:, :count, vocab:] = extra.astype(BF16).reshape(NX, count, 128)
    out[:, count:, :] = below[...]


def head(own, other, w_own, w_other, below):
    vocab = w_own.shape[1]
    total = own.shape[0] * own.shape[1] * own.shape[2]
    rows = total // NX + below.shape[1]
    return pl.pallas_call(
        head_kernel,
        out_shape=pltpu.HBM((NX, rows, vocab + 128), BF16),
        compiler_params=pltpu.CompilerParams(vmem_limit_bytes=32 << 20),
        cost_estimate=pl.CostEstimate(
            flops=4 * total * own.shape[3] * vocab, bytes_accessed=4 << 20, transcendentals=0
        ),
        name="head",
    )(own, other, w_own, w_other, below)


def finish_kernel(place, parts, token, stats):
    count = token.shape[0]
    vocab = parts.shape[2] - 128
    total = jnp.sum(parts[:, :count, :].astype(F32), axis=0)
    square = jnp.sum(total[:, vocab:], axis=1, keepdims=True)
    logits = total[:, :vocab] * lax.rsqrt(square / place[1] + EPS)
    top = jnp.max(logits, axis=1, keepdims=True)
    summed = jnp.sum(jnp.exp(logits - top), axis=1, keepdims=True)
    slice_width = vocab // NX
    local = token[...] - place[0] * slice_width
    block = NZ * NY * NC * slice_width
    lanes = lax.broadcasted_iota(jnp.int32, logits.shape, 1)
    entry = (lanes // slice_width) * block + lanes % slice_width
    chosen = jnp.sum(jnp.where(entry == local, logits, 0.0), axis=1, keepdims=True)
    lane = lax.broadcasted_iota(jnp.int32, stats.shape, 1)
    stats[...] = jnp.where(lane == 0, top, jnp.where(lane == 1, summed, chosen))


def finish(place, parts, token):
    return pl.pallas_call(
        finish_kernel,
        out_shape=jax.ShapeDtypeStruct((token.shape[0], 128), F32),
        in_specs=[
            pl.BlockSpec(memory_space=pltpu.SMEM),
            pl.BlockSpec(memory_space=pltpu.VMEM),
            pl.BlockSpec(memory_space=pltpu.VMEM),
        ],
        compiler_params=pltpu.CompilerParams(vmem_limit_bytes=32 << 20),
        name="finish",
    )(place, parts, token)


def shards(
    queries,
    new_keys,
    new_values,
    k_cache,
    v_cache,
    lengths,
    residual,
    w_out,
    router,
    gain_moe,
    w_gate,
    w_up,
    w_down,
    expert_ids,
    gain_final,
    w_vocab,
    tokens,
    mu,
):
    x, z, y, core = (lax.axis_index(name) for name in ("x", "z", "y", "c"))
    expert = y * NC + core
    place = jnp.stack([expert, core, x]).astype(jnp.int32)
    width_all = gain_moe.shape[0]
    unit = w_out.shape[1]
    total_rows = residual.shape[0]
    part_rows = total_rows // (NX * NY * NC)

    sends = pack(place, w_out.T, residual.T, part_rows)
    *sends, queries = lax.optimization_barrier((*sends, queries))
    packs = [sends[0]]
    for shift in range(1, NX):
        pairs = [(i, (i + shift) % NX) for i in range(NX)]
        packs.append(lax.ppermute(sends[shift], "x", pairs))

    attended = attend(queries, new_keys, new_values, k_cache, v_cache, lengths)
    attended_x = exchange(attended, "z")
    partial_heads, residual_here = project(place, attended_x, packs)
    partial_heads, w_vocab = lax.optimization_barrier((partial_heads, w_vocab))
    half = width_all // NC
    slab = half // NX
    vocab_rows = w_vocab.reshape(NC, NX, slab, -1)
    vocab_parts = []
    for shift in range(NX):
        part = lax.dynamic_index_in_dim(vocab_rows, (x + shift) % NX, 1, keepdims=False)
        if shift:
            part = lax.ppermute(part, "x", [(i, (i + shift) % NX) for i in range(NX)])
        vocab_parts.append(part)
    gain_slab = gain_final.reshape(NC, NX, slab)
    gain_slab = lax.dynamic_index_in_dim(gain_slab, x, 1, keepdims=False)[:, :, None]
    columns = []
    for i in range(NX):
        away = (x - i) % NX
        part = vocab_parts[NX - 1]
        for shift in range(NX - 1):
            part = jnp.where(away == shift, vocab_parts[shift], part)
        columns.append((part.astype(F32) * gain_slab).astype(BF16))
    head_w = jnp.concatenate(columns, axis=2)
    head_own = lax.dynamic_index_in_dim(head_w, core, 0, keepdims=False)
    head_other = lax.dynamic_index_in_dim(head_w, 1 - core, 0, keepdims=False)

    pieces = exchange(partial_heads, EX)
    hidden = jnp.sum(pieces.astype(F32), axis=0) + residual_here.astype(F32)
    hidden = hidden.astype(BF16)

    hidden_z = spread(hidden, "z", NZ)
    early = (hidden_z, head_own, head_other, expert_ids, w_gate, w_up, w_down, router)
    early = lax.optimization_barrier(early)
    hidden_z, head_own, head_other, expert_ids, w_gate, w_up, w_down, router = early
    own = spread(hidden_z, XY, NXY)
    order = expert_ids.reshape(NXY, NC, part_rows, 2).transpose(1, 0, 2, 3)
    order = order.reshape(NC, -1, 2)
    order_own = lax.dynamic_index_in_dim(order, core, 0, keepdims=False)
    order_other = lax.dynamic_index_in_dim(order, 1 - core, 0, keepdims=False)
    gain_col = gain_moe[:, None]
    router_g = (router.astype(F32) * gain_col).astype(BF16)
    router_z = router_g.T.reshape(-1, NX, NZ, unit).transpose(2, 0, 1, 3)
    router_z = router_z.reshape(NZ, -1, NX * unit)
    gate_g = (w_gate[0].astype(F32) * gain_col).astype(BF16)
    up_g = (w_up[0].astype(F32) * gain_col).astype(BF16)
    down_sent = lax.dynamic_slice_in_dim(w_down[0], (1 - core) * half, half, axis=1)
    down_other = swap_cores(down_sent)
    ready = (own, gate_g, up_g, router_z, order_own, order_other, down_other)
    ready = lax.optimization_barrier(ready)
    own, gate_g, up_g, router_z, order_own, order_other, down_other = ready
    other = swap_cores(own)

    act_own = experts(place, own, gate_g, up_g, router_z, order_own)
    act_other = experts(place, other, gate_g, up_g, router_z, order_other)
    acts = (act_own, act_other, swap_cores(act_other), swap_cores(act_own))
    sent = down(place, acts, w_down[0], down_other)
    sent = sent.reshape(NXY, NZ, part_rows, slab)
    sums = jnp.sum(exchange(sent, XY).astype(F32), axis=0).astype(BF16)
    sums = jnp.sum(exchange(sums, "z").astype(F32), axis=0)

    units = slab // unit
    first_unit = core * (half // unit) + x * units
    start = (y * NX + z // 2, first_unit % NZ, 0, 0)
    size = (1, units, part_rows, NX * unit)
    rows_here = jnp.where(
        z % 2 == core, lax.dynamic_slice(own, start, size), lax.dynamic_slice(other, start, size)
    )[0].reshape(units, part_rows, NX, unit)
    cut = lax.dynamic_index_in_dim(rows_here, first_unit // NZ, 2, keepdims=False)
    hidden_here = cut.transpose(1, 0, 2).reshape(part_rows, slab).astype(F32)
    moved = (hidden_here + sums).astype(BF16)

    final_own = spread(spread(moved, "z", NZ), "y", NY).reshape(NY, NZ, part_rows, slab)
    final_other = swap_cores(final_own)
    count = total_rows // NX

    own_rows = total_rows // (NX * NZ * NY * NC)
    size = (NX, 1, own_rows, slab)
    start = (0, z, expert * own_rows, 0)
    near = lax.dynamic_slice(final_own, start, size)
    far = lax.dynamic_slice(final_other, start, size)
    low = jnp.where(core == 0, near, far)
    high = jnp.where(core == 0, far, near)
    vocab = head_own.shape[1]
    rows_out = jnp.concatenate([low, high], axis=1).reshape(NX, -1, vocab)
    below = jnp.pad(rows_out, ((0, 0), (0, 16 - rows_out.shape[1]), (0, 128)))
    partial = head(final_own, final_other, head_own, head_other, below)
    parts = exchange(partial, "x")
    hidden_out = parts[:, count : count + rows_out.shape[1], :vocab]
    hidden_out = hidden_out.reshape(NX, NC, own_rows, slab).transpose(2, 1, 0, 3)
    hidden_out = hidden_out.reshape(own_rows, width_all)

    token = lax.dynamic_slice_in_dim(tokens, x * count, count)[:, None]
    where = jnp.stack([z * (NY * NC) + expert, jnp.int32(width_all)]).astype(jnp.int32)
    stats = finish(where, parts, token)
    flat = stats[:, :4].reshape(-1, own_rows * 4)
    flat = jnp.pad(flat, ((0, 0), (0, 128 - own_rows * 4)))
    got = exchange(flat, ("z", "y", "c"))[:, : own_rows * 4].reshape(-1, own_rows, 4)
    top = jnp.max(got[:, :, 0], axis=0)
    summed_all = jnp.sum(got[:, :, 1] * jnp.exp(got[:, :, 0] - top[None]), axis=0)
    chosen = jnp.sum(got[:, :, 2], axis=0)
    surprise = (top + jnp.log(summed_all) - chosen) / LOG_TWO
    mu_next = mu - RATE * (surprise - TARGET)
    return (hidden_out, surprise, mu_next)


def solution(mesh):
    fine = Mesh(mesh.devices.reshape(NX, NZ, NY, NC), ALL)
    dp = ("x", "z")
    return jax.shard_map(
        shards,
        mesh=fine,
        in_specs=(
            P(dp, EX),
            P(dp, EX),
            P(dp, EX),
            P(dp, EX, None, None),
            P(dp, EX, None, None),
            P(dp),
            P(None, dp),
            P(EX, dp),
            P(),
            P(),
            P(EX, None, dp),
            P(EX, None, dp),
            P(EX, dp, None),
            P(),
            P(),
            P(None, ALL),
            P(),
            P(ALL),
        ),
        out_specs=(P(ALL, None), P(ALL), P(ALL)),
        check_vma=False,
    )
```

```python
import jax
import jax.numpy as jnp
from jax import lax
from jax.experimental import pallas as pl
from jax.experimental.pallas import tpu as pltpu
from jax.sharding import Mesh
from jax.sharding import PartitionSpec as P

EPS = 1e-05
TARGET = 5.0
RATE = 0.1
LOG_TWO = 0.6931471805599453
F32 = jnp.float32
BF16 = jnp.bfloat16
NX, NZ, NY, NC = 4, 8, 4, 2
NXY = NX * NY
XY = ("x", "y")
EX = ("y", "c")
ALL = ("x", "z", "y", "c")


def whole(shape):
    return pl.BlockSpec(shape, lambda *_: (0,) * len(shape))


def swap_cores(value):
    return lax.ppermute(value, "c", [(0, 1), (1, 0)])


def exchange(value, axes):
    return lax.all_to_all(value, axes, split_axis=0, concat_axis=0, tiled=True)


def spread(value, axes, count):
    return exchange(jnp.broadcast_to(value[None], (count,) + value.shape), axes)


def attend_kernel(lengths, queries, new_keys, new_values, k_cache, v_cache, out):
    rows, _, span, width = k_cache.shape
    group = queries.shape[1] // width
    total = group * rows
    query = jnp.concatenate(
        [queries[:, h * width : (h + 1) * width] for h in range(group)], axis=0
    )
    scale = width ** (-0.5)
    keys = k_cache[...].reshape(rows * span, width)
    scores = (
        lax.dot_general(query, keys, (((1,), (1,)), ((), ())), preferred_element_type=F32) * scale
    )
    fresh_key = jnp.concatenate([new_keys[...].astype(F32)] * group, axis=0)
    fresh = jnp.sum(query.astype(F32) * fresh_key, axis=1, keepdims=True) * scale
    request = lax.broadcasted_iota(jnp.int32, (total, 1), 0) % rows
    first = request * span
    last = first
    for r in range(rows):
        last = jnp.where(request == r, r * span + lengths[r], last)
    column = lax.broadcasted_iota(jnp.int32, scores.shape, 1)
    scores = jnp.where((column >= first) & (column < last), scores, -1e30)
    top = jnp.maximum(jnp.max(scores, axis=1, keepdims=True), fresh)
    part = jnp.exp(scores - top)
    part_fresh = jnp.exp(fresh - top)
    sums = jnp.sum(part, axis=1, keepdims=True) + part_fresh
    weight = (part / sums).astype(BF16)
    weight_fresh = (part_fresh / sums).astype(BF16).astype(F32)
    values = v_cache[...].reshape(rows * span, width)
    result = jnp.dot(weight, values, preferred_element_type=F32)
    fresh_value = jnp.concatenate([new_values[...].astype(F32)] * group, axis=0)
    result = (result + weight_fresh * fresh_value).astype(BF16)
    wide = jnp.concatenate([result[h * rows : (h + 1) * rows] for h in range(group)], axis=1)
    for z in range(out.shape[0]):
        out[z] = wide


def attend(queries, new_keys, new_values, k_cache, v_cache, lengths):
    rows, width = queries.shape
    arrays = (queries, new_keys, new_values, k_cache, v_cache)
    return pl.pallas_call(
        attend_kernel,
        out_shape=pltpu.HBM((NZ, rows, width), BF16),
        grid=(1,),
        in_specs=[pl.BlockSpec(memory_space=pltpu.SMEM)] + [whole(a.shape) for a in arrays],
        out_specs=whole((NZ, rows, width)),
        compiler_params=pltpu.CompilerParams(vmem_limit_bytes=32 << 20),
        cost_estimate=pl.CostEstimate(flops=2 << 34, bytes_accessed=2 << 20, transcendentals=0),
        name="attend",
    )(lengths, *arrays)


def pack_kernel(place, w_out, residual, *packs):
    unit, depth = w_out.shape
    rows = packs[0].shape[0] - unit
    line = lax.broadcasted_iota(jnp.int32, (NX * rows, residual.shape[1]), 0)
    target = lax.rem(place[2] + line // rows, NX)
    wanted = (target * NY * NC + place[0]) * rows + line % rows
    pick = lax.broadcasted_iota(jnp.int32, line.shape, 1) == wanted
    parts = lax.dot_general(
        pick.astype(F32).astype(BF16),
        residual[...],
        (((1,), (1,)), ((), ())),
        preferred_element_type=F32,
    )
    for shift, pack in enumerate(packs):
        part = parts[shift * rows : (shift + 1) * rows, :]
        pack[:unit, :] = w_out[...]
        pack[unit:, :] = jnp.concatenate(
            [part, jnp.zeros((rows, depth - unit), F32)], axis=1
        ).astype(BF16)


def pack(place, w_out, residual, rows):
    unit, depth = w_out.shape
    shape = (unit + rows, depth)
    return pl.pallas_call(
        pack_kernel,
        out_shape=[jax.ShapeDtypeStruct(shape, BF16)] + [pltpu.HBM(shape, BF16)] * (NX - 1),
        grid=(1,),
        in_specs=[
            pl.BlockSpec(memory_space=pltpu.SMEM),
            whole(w_out.shape),
            whole(residual.shape),
        ],
        out_specs=[whole(shape)] * NX,
        compiler_params=pltpu.CompilerParams(vmem_limit_bytes=32 << 20),
        name="pack",
    )(place, w_out, residual)


def project_kernel(place, attended, *refs):
    packs, (partial, residual) = refs[:NX], refs[NX:]
    depth = attended.shape[-1]
    value = attended[...].reshape(-1, depth)
    unit = residual.shape[1] // NX
    products = [
        lax.dot_general(
            value, pack[:unit, :], (((1,), (1,)), ((), ())), preferred_element_type=F32
        )
        for pack in packs
    ]
    rows = [pack[unit:, :].astype(F32)[:, :unit] for pack in packs]
    x = place[2]

    def order(parts):
        blocks = []
        for i in range(NX):
            away = lax.rem(x - i + NX, NX)
            block = parts[NX - 1]
            for shift in range(NX - 1):
                block = jnp.where(away == shift, parts[shift], block)
            blocks.append(block)
        return jnp.concatenate(blocks, axis=1).astype(BF16)

    partial[...] = order(products).reshape(partial.shape)
    residual[...] = order(rows)


def project(place, attended, packs):
    _, rows, depth = attended.shape
    unit = packs[0].shape[0] - rows
    vmem = pl.BlockSpec(memory_space=pltpu.VMEM)
    return pl.pallas_call(
        project_kernel,
        out_shape=(
            jax.ShapeDtypeStruct((NY * NC, rows, NX * unit), BF16),
            jax.ShapeDtypeStruct((rows, NX * unit), BF16),
        ),
        in_specs=[pl.BlockSpec(memory_space=pltpu.SMEM)] + [vmem] * (1 + NX),
        out_specs=(vmem, vmem),
        compiler_params=pltpu.CompilerParams(vmem_limit_bytes=32 << 20),
        cost_estimate=pl.CostEstimate(
            flops=2 * NZ * rows * depth * NX * unit, bytes_accessed=2 << 20, transcendentals=0
        ),
        name="project",
    )(place, attended, *packs)


def expert_kernel(
    place, own, other, gate_w, up_w, router_w, ids, act, gate_sum, up_sum, route_sum, squares
):
    step = pl.program_id(0)
    width = own.shape[-1]

    def products(state):
        gate = up = route = square = 0.0
        for block in range(state.shape[1]):
            hidden = state[:, block].reshape(-1, width)
            gate += jnp.dot(
                hidden, gate_w[:, block].reshape(width, -1), preferred_element_type=F32
            )
            up += jnp.dot(hidden, up_w[:, block].reshape(width, -1), preferred_element_type=F32)
            route += lax.dot_general(
                hidden, router_w[block], (((1,), (1,)), ((), ())), preferred_element_type=F32
            )
            wide = hidden.astype(F32)
            for start in range(0, width, 128):
                piece = wide[:, start : start + 128]
                square += piece * piece
        return gate, up, route, square

    @pl.when(step == 0)
    def _():
        gate_sum[...], up_sum[...], route_sum[...], squares[...] = products(own)

    @pl.when(step == 1)
    def _():
        gate, up, route, square = products(other)
        square += squares[...]
        mean = jnp.sum(square, axis=1, keepdims=True) / (width * NZ)
        scale = lax.rsqrt(mean + EPS)
        logits = (route + route_sum[...]) * scale
        lanes = lax.broadcasted_iota(jnp.int32, logits.shape, 1)
        first = ids[:, 0:1]
        second = ids[:, 1:2]
        first_logit = jnp.sum(jnp.where(lanes == first, logits, 0.0), axis=1, keepdims=True)
        second_logit = jnp.sum(jnp.where(lanes == second, logits, 0.0), axis=1, keepdims=True)
        expert = place[0]
        is_first = first == expert
        gap = second_logit - first_logit
        weight = 1.0 / (1.0 + jnp.exp(jnp.where(is_first, gap, -gap)))
        weight = jnp.where(is_first | (second == expert), weight, 0.0)
        gated = (gate + gate_sum[...]) * scale
        value = jax.nn.silu(gated) * ((up + up_sum[...]) * scale)
        act[...] = (weight * value).astype(BF16)


def experts(place, own, other, gate_w, up_w, router_w, ids):
    _, step, rows, width = own.shape
    total = NXY * rows
    hidden_units = gate_w.shape[-1]
    unit = width // NX
    count = router_w.shape[1]

    def half(s, p):
        return p[1] + s - 2 * p[1] * s

    weights = pl.BlockSpec(
        (NX, step, unit, hidden_units), lambda s, p: (0, half(s, p), 0, 0)
    )
    return pl.pallas_call(
        expert_kernel,
        out_shape=jax.ShapeDtypeStruct((total, hidden_units), BF16),
        grid_spec=pltpu.PrefetchScalarGridSpec(
            num_scalar_prefetch=1,
            grid=(NC,),
            in_specs=[
                whole(own.shape),
                whole(other.shape),
                weights,
                weights,
                pl.BlockSpec((step, count, width), lambda s, p: (half(s, p), 0, 0)),
                whole(ids.shape),
            ],
            out_specs=whole((total, hidden_units)),
            scratch_shapes=[
                pltpu.VMEM((total, hidden_units), F32),
                pltpu.VMEM((total, hidden_units), F32),
                pltpu.VMEM((total, count), F32),
                pltpu.VMEM((total, 128), F32),
            ],
        ),
        compiler_params=pltpu.CompilerParams(
            dimension_semantics=("arbitrary",), vmem_limit_bytes=32 << 20
        ),
        cost_estimate=pl.CostEstimate(
            flops=2 * total * width * NZ * 2 * hidden_units,
            bytes_accessed=10 << 20,
            transcendentals=total * hidden_units,
        ),
        name="experts",
    )(
        place,
        own,
        other,
        gate_w.reshape(NX, NZ, unit, hidden_units),
        up_w.reshape(NX, NZ, unit, hidden_units),
        router_w,
        ids,
    )


def down_kernel(place, mine, theirs, w_mine, w_theirs, out):
    total = jnp.dot(mine[...], w_mine[...], preferred_element_type=F32)
    total += jnp.dot(theirs[...], w_theirs[...], preferred_element_type=F32)
    out[0] = total.astype(BF16).reshape(out.shape[1:])


def down(place, mine, theirs, w_mine, w_theirs):
    total, units = mine.shape
    rows = total // NXY
    width = w_theirs.shape[1] // NX
    return pl.pallas_call(
        down_kernel,
        out_shape=pltpu.HBM((NX, NXY, rows, width), BF16),
        grid_spec=pltpu.PrefetchScalarGridSpec(
            num_scalar_prefetch=1,
            grid=(NX,),
            in_specs=[
                whole(mine.shape),
                whole(theirs.shape),
                pl.BlockSpec((units, width), lambda x, p: (0, p[1] * NX + x)),
                pl.BlockSpec((units, width), lambda x, p: (0, x)),
            ],
            out_specs=pl.BlockSpec((1, NXY, rows, width), lambda x, p: (x, 0, 0, 0)),
        ),
        compiler_params=pltpu.CompilerParams(
            dimension_semantics=("arbitrary",), vmem_limit_bytes=32 << 20
        ),
        cost_estimate=pl.CostEstimate(
            flops=4 * total * units * width * NX, bytes_accessed=5 << 20, transcendentals=0
        ),
        name="down",
    )(place, mine, theirs, w_mine, w_theirs)


def head_kernel(own, other, w_own, w_other, below, out):
    width = own.shape[-1]
    vocab = w_own.shape[1]
    near = own[...].reshape(-1, width)
    far = other[...].reshape(-1, width)
    logits = jnp.dot(near, w_own[...], preferred_element_type=F32)
    logits += jnp.dot(far, w_other[...], preferred_element_type=F32)
    square = jnp.zeros((near.shape[0], 128), F32)
    for part in (near.astype(F32), far.astype(F32)):
        for start in range(0, width, 128):
            piece = part[:, start : start + 128]
            square += piece * piece
    square = jnp.sum(square, axis=1, keepdims=True)
    high = square.astype(BF16).astype(F32)
    lanes = lax.broadcasted_iota(jnp.int32, (near.shape[0], 128), 1)
    extra = jnp.where(lanes == 0, high, jnp.where(lanes == 1, square - high, 0.0))
    count = near.shape[0] // NX
    out[:, :count, :vocab] = logits.astype(BF16).reshape(NX, count, vocab)
    out[:, :count, vocab:] = extra.astype(BF16).reshape(NX, count, 128)
    out[:, count:, :] = below[...]


def head(own, other, w_own, w_other, below):
    vocab = w_own.shape[1]
    total = own.shape[0] * own.shape[1] * own.shape[2]
    rows = total // NX + below.shape[1]
    return pl.pallas_call(
        head_kernel,
        out_shape=pltpu.HBM((NX, rows, vocab + 128), BF16),
        compiler_params=pltpu.CompilerParams(vmem_limit_bytes=32 << 20),
        cost_estimate=pl.CostEstimate(
            flops=4 * total * own.shape[3] * vocab, bytes_accessed=4 << 20, transcendentals=0
        ),
        name="head",
    )(own, other, w_own, w_other, below)


def finish_kernel(place, parts, token, stats):
    count = token.shape[0]
    vocab = parts.shape[2] - 128
    total = jnp.sum(parts[:, :count, :].astype(F32), axis=0)
    square = jnp.sum(total[:, vocab:], axis=1, keepdims=True)
    logits = total[:, :vocab] * lax.rsqrt(square / place[1] + EPS)
    top = jnp.max(logits, axis=1, keepdims=True)
    summed = jnp.sum(jnp.exp(logits - top), axis=1, keepdims=True)
    slice_width = vocab // NX
    local = token[...] - place[0] * slice_width
    block = NZ * NY * NC * slice_width
    lanes = lax.broadcasted_iota(jnp.int32, logits.shape, 1)
    entry = (lanes // slice_width) * block + lanes % slice_width
    chosen = jnp.sum(jnp.where(entry == local, logits, 0.0), axis=1, keepdims=True)
    lane = lax.broadcasted_iota(jnp.int32, stats.shape, 1)
    stats[...] = jnp.where(lane == 0, top, jnp.where(lane == 1, summed, chosen))


def finish(place, parts, token):
    return pl.pallas_call(
        finish_kernel,
        out_shape=jax.ShapeDtypeStruct((token.shape[0], 128), F32),
        in_specs=[
            pl.BlockSpec(memory_space=pltpu.SMEM),
            pl.BlockSpec(memory_space=pltpu.VMEM),
            pl.BlockSpec(memory_space=pltpu.VMEM),
        ],
        compiler_params=pltpu.CompilerParams(vmem_limit_bytes=32 << 20),
        name="finish",
    )(place, parts, token)


def shards(
    queries,
    new_keys,
    new_values,
    k_cache,
    v_cache,
    lengths,
    residual,
    w_out,
    router,
    gain_moe,
    w_gate,
    w_up,
    w_down,
    expert_ids,
    gain_final,
    w_vocab,
    tokens,
    mu,
):
    x, z, y, core = (lax.axis_index(name) for name in ("x", "z", "y", "c"))
    expert = y * NC + core
    place = jnp.stack([expert, core, x]).astype(jnp.int32)
    width_all = gain_moe.shape[0]
    unit = w_out.shape[1]
    total_rows = residual.shape[0]
    part_rows = total_rows // (NX * NY * NC)

    sends = pack(place, w_out.T, residual.T, part_rows)
    *sends, queries = lax.optimization_barrier((*sends, queries))
    packs = [sends[0]]
    for shift in range(1, NX):
        pairs = [(i, (i + shift) % NX) for i in range(NX)]
        packs.append(lax.ppermute(sends[shift], "x", pairs))

    attended = attend(queries, new_keys, new_values, k_cache, v_cache, lengths)
    attended_x = exchange(attended, "z")
    partial_heads, residual_here = project(place, attended_x, packs)
    half = width_all // NC
    slab = half // NX
    pieces = exchange(partial_heads, EX)
    hidden = jnp.sum(pieces.astype(F32), axis=0) + residual_here.astype(F32)
    hidden = hidden.astype(BF16)

    hidden_z = spread(hidden, "z", NZ)
    depth_z = NZ // NC
    near = lax.dynamic_slice_in_dim(hidden_z, core * depth_z, depth_z)
    far = swap_cores(lax.dynamic_slice_in_dim(hidden_z, (1 - core) * depth_z, depth_z))
    chunks = [jnp.where(core == k, near, far) for k in range(NC)]

    early = (*chunks, expert_ids, w_gate, w_up, w_down, router)
    early = lax.optimization_barrier(early)
    chunks = list(early[:NC])
    expert_ids, w_gate, w_up, w_down, router = early[NC:]
    own = [spread(chunks[0], XY, NXY)]
    order = expert_ids.reshape(NXY, NC, part_rows, 2).transpose(1, 0, 2, 3)
    order = order.reshape(NC, -1, 2)
    gain_col = gain_moe[:, None]
    router_g = (router.astype(F32) * gain_col).astype(BF16)
    router_z = router_g.T.reshape(-1, NX, NZ, unit).transpose(2, 0, 1, 3)
    router_z = router_z.reshape(NZ, -1, NX * unit)
    gate_g = (w_gate[0].astype(F32) * gain_col).astype(BF16)
    up_g = (w_up[0].astype(F32) * gain_col).astype(BF16)
    down_sent = lax.dynamic_slice_in_dim(w_down[0], (1 - core) * half, half, axis=1)
    down_other = swap_cores(down_sent)
    ready = (own[0], chunks[1], gate_g, up_g, router_z, order, down_other)
    ready = lax.optimization_barrier(ready)
    own[0], chunks[1], gate_g, up_g, router_z, order, down_other = ready
    own.append(spread(chunks[1], XY, NXY))
    other = []
    sums = []
    for k in range(NC):
        other.append(swap_cores(own[k]))
        act = experts(place, own[k], other[k], gate_g, up_g, router_z, order[k])
        sent = down(place, act, swap_cores(act), w_down[0], down_other)
        if k == 0:
            own[1], sent = lax.optimization_barrier((own[1], sent))
        sent = sent.reshape(NXY, NZ // NC, part_rows, slab)
        sums.append(jnp.sum(exchange(sent, XY).astype(F32), axis=0).astype(BF16))
    sums = jnp.stack(sums, axis=1).reshape(NZ, part_rows, slab)
    sums, w_vocab = lax.optimization_barrier((sums, w_vocab))
    vocab_rows = w_vocab.reshape(NC, NX, slab, -1)
    vocab_parts = []
    for shift in range(NX):
        part = lax.dynamic_index_in_dim(vocab_rows, (x + shift) % NX, 1, keepdims=False)
        if shift:
            part = lax.ppermute(part, "x", [(i, (i + shift) % NX) for i in range(NX)])
        vocab_parts.append(part)
    gain_slab = gain_final.reshape(NC, NX, slab)
    gain_slab = lax.dynamic_index_in_dim(gain_slab, x, 1, keepdims=False)[:, :, None]
    columns = []
    for i in range(NX):
        away = (x - i) % NX
        part = vocab_parts[NX - 1]
        for shift in range(NX - 1):
            part = jnp.where(away == shift, vocab_parts[shift], part)
        columns.append((part.astype(F32) * gain_slab).astype(BF16))
    head_w = jnp.concatenate(columns, axis=2)
    head_own = lax.dynamic_index_in_dim(head_w, core, 0, keepdims=False)
    head_other = lax.dynamic_index_in_dim(head_w, 1 - core, 0, keepdims=False)

    sums = jnp.sum(exchange(sums, "z").astype(F32), axis=0)

    units = slab // unit
    first_unit = core * (half // unit) + x * units
    here = [
        lax.dynamic_index_in_dim(a, y * NX + z // 2, 0, keepdims=False) for a in (*own, *other)
    ]
    inner = x % 2 == core
    rows_here = jnp.where(
        z % 2 == 0,
        jnp.where(inner, here[0], here[NC]),
        jnp.where(inner, here[1], here[NC + 1]),
    ).reshape(units, part_rows, NX, unit)
    cut = lax.dynamic_index_in_dim(rows_here, first_unit // NZ, 2, keepdims=False)
    hidden_here = cut.transpose(1, 0, 2).reshape(part_rows, slab).astype(F32)
    moved = (hidden_here + sums).astype(BF16)

    moved_z = spread(moved, "z", NZ)
    moved_z, head_own, head_other = lax.optimization_barrier((moved_z, head_own, head_other))
    final_own = spread(moved_z, "y", NY).reshape(NY, NZ, part_rows, slab)
    final_other = swap_cores(final_own)
    count = total_rows // NX

    own_rows = total_rows // (NX * NZ * NY * NC)
    size = (NX, 1, own_rows, slab)
    start = (0, z, expert * own_rows, 0)
    near = lax.dynamic_slice(final_own, start, size)
    far = lax.dynamic_slice(final_other, start, size)
    low = jnp.where(core == 0, near, far)
    high = jnp.where(core == 0, far, near)
    vocab = head_own.shape[1]
    rows_out = jnp.concatenate([low, high], axis=1).reshape(NX, -1, vocab)
    below = jnp.pad(rows_out, ((0, 0), (0, 16 - rows_out.shape[1]), (0, 128)))
    partial = head(final_own, final_other, head_own, head_other, below)
    parts = exchange(partial, "x")
    hidden_out = parts[:, count : count + rows_out.shape[1], :vocab]
    hidden_out = hidden_out.reshape(NX, NC, own_rows, slab).transpose(2, 1, 0, 3)
    hidden_out = hidden_out.reshape(own_rows, width_all)

    token = lax.dynamic_slice_in_dim(tokens, x * count, count)[:, None]
    where = jnp.stack([z * (NY * NC) + expert, jnp.int32(width_all)]).astype(jnp.int32)
    stats = finish(where, parts, token)
    flat = stats[:, :4].reshape(-1, own_rows * 4)
    flat = jnp.pad(flat, ((0, 0), (0, 128 - own_rows * 4)))
    got = exchange(flat, ("z", "y", "c"))[:, : own_rows * 4].reshape(-1, own_rows, 4)
    top = jnp.max(got[:, :, 0], axis=0)
    summed_all = jnp.sum(got[:, :, 1] * jnp.exp(got[:, :, 0] - top[None]), axis=0)
    chosen = jnp.sum(got[:, :, 2], axis=0)
    surprise = (top + jnp.log(summed_all) - chosen) / LOG_TWO
    mu_next = mu - RATE * (surprise - TARGET)
    return (hidden_out, surprise, mu_next)


def solution(mesh):
    fine = Mesh(mesh.devices.reshape(NX, NZ, NY, NC), ALL)
    dp = ("x", "z")
    return jax.shard_map(
        shards,
        mesh=fine,
        in_specs=(
            P(dp, EX),
            P(dp, EX),
            P(dp, EX),
            P(dp, EX, None, None),
            P(dp, EX, None, None),
            P(dp),
            P(None, dp),
            P(EX, dp),
            P(),
            P(),
            P(EX, None, dp),
            P(EX, None, dp),
            P(EX, dp, None),
            P(),
            P(),
            P(None, ALL),
            P(),
            P(ALL),
        ),
        out_specs=(P(ALL, None), P(ALL), P(ALL)),
        check_vma=False,
    )
```

```python
import jax
import jax.numpy as jnp
from jax import lax
from jax.experimental import pallas as pl
from jax.experimental.pallas import tpu as pltpu
from jax.sharding import Mesh
from jax.sharding import PartitionSpec as P

EPS = 1e-05
TARGET = 5.0
RATE = 0.1
LOG_TWO = 0.6931471805599453
F32 = jnp.float32
BF16 = jnp.bfloat16
NX, NZ, NY, NC = 4, 8, 4, 2
NXY = NX * NY
XY = ("x", "y")
EX = ("y", "c")
ALL = ("x", "z", "y", "c")


def whole(shape):
    return pl.BlockSpec(shape, lambda *_: (0,) * len(shape))


HBM = pl.BlockSpec(memory_space=pltpu.HBM)


def fetch(sources, buffers, sems):
    copies = [
        pltpu.make_async_copy(source, buffer, sems.at[i])
        for i, (source, buffer) in enumerate(zip(sources, buffers))
    ]
    for copy in copies:
        copy.start()
    for copy in copies:
        copy.wait()


def buffers_for(arrays):
    return [pltpu.VMEM(a.shape, a.dtype) for a in arrays] + [
        pltpu.SemaphoreType.DMA((len(arrays),))
    ]


def swap_cores(value):
    return lax.ppermute(value, "c", [(0, 1), (1, 0)])


def exchange(value, axes):
    return lax.all_to_all(value, axes, split_axis=0, concat_axis=0, tiled=True)


def spread(value, axes, count):
    return exchange(jnp.broadcast_to(value[None], (count,) + value.shape), axes)


def attend_kernel(lengths, *refs):
    out = refs[5]
    fetch(refs[:5], refs[6:11], refs[11])
    queries, new_keys, new_values, k_cache, v_cache = refs[6:11]
    rows, _, span, width = k_cache.shape
    group = queries.shape[1] // width
    total = group * rows
    query = jnp.concatenate(
        [queries[:, h * width : (h + 1) * width] for h in range(group)], axis=0
    )
    scale = width ** (-0.5)
    keys = k_cache[...].reshape(rows * span, width)
    scores = (
        lax.dot_general(query, keys, (((1,), (1,)), ((), ())), preferred_element_type=F32) * scale
    )
    fresh_key = jnp.concatenate([new_keys[...].astype(F32)] * group, axis=0)
    fresh = jnp.sum(query.astype(F32) * fresh_key, axis=1, keepdims=True) * scale
    request = lax.broadcasted_iota(jnp.int32, (total, 1), 0) % rows
    first = request * span
    last = first
    for r in range(rows):
        last = jnp.where(request == r, r * span + lengths[r], last)
    column = lax.broadcasted_iota(jnp.int32, scores.shape, 1)
    scores = jnp.where((column >= first) & (column < last), scores, -1e30)
    top = jnp.maximum(jnp.max(scores, axis=1, keepdims=True), fresh)
    part = jnp.exp(scores - top)
    part_fresh = jnp.exp(fresh - top)
    sums = jnp.sum(part, axis=1, keepdims=True) + part_fresh
    weight = (part / sums).astype(BF16)
    weight_fresh = (part_fresh / sums).astype(BF16).astype(F32)
    values = v_cache[...].reshape(rows * span, width)
    result = jnp.dot(weight, values, preferred_element_type=F32)
    fresh_value = jnp.concatenate([new_values[...].astype(F32)] * group, axis=0)
    result = (result + weight_fresh * fresh_value).astype(BF16)
    wide = jnp.concatenate([result[h * rows : (h + 1) * rows] for h in range(group)], axis=1)
    for z in range(out.shape[0]):
        out[z] = wide


def attend(queries, new_keys, new_values, k_cache, v_cache, lengths):
    rows, width = queries.shape
    arrays = (queries, new_keys, new_values, k_cache, v_cache)
    return pl.pallas_call(
        attend_kernel,
        out_shape=pltpu.HBM((NZ, rows, width), BF16),
        grid=(1,),
        in_specs=[pl.BlockSpec(memory_space=pltpu.SMEM)] + [HBM] * len(arrays),
        out_specs=whole((NZ, rows, width)),
        scratch_shapes=buffers_for(arrays),
        compiler_params=pltpu.CompilerParams(vmem_limit_bytes=60 << 20),
        cost_estimate=pl.CostEstimate(flops=2 << 34, bytes_accessed=2 << 20, transcendentals=0),
        name="attend",
    )(lengths, *arrays)


def pack_kernel(place, *refs):
    packs = refs[2 : 2 + NX]
    w_out, residual, sems = refs[2 + NX :]
    fetch(refs[:2], (w_out, residual), sems)
    unit, depth = w_out.shape
    rows = packs[0].shape[0] - unit
    line = lax.broadcasted_iota(jnp.int32, (NX * rows, residual.shape[1]), 0)
    target = lax.rem(place[2] + line // rows, NX)
    wanted = (target * NY + place[0] // NC) * rows + line % rows
    pick = lax.broadcasted_iota(jnp.int32, line.shape, 1) == wanted
    parts = lax.dot_general(
        pick.astype(F32).astype(BF16),
        residual[...],
        (((1,), (1,)), ((), ())),
        preferred_element_type=F32,
    )
    for shift, pack in enumerate(packs):
        part = parts[shift * rows : (shift + 1) * rows, :]
        pack[:unit, :] = w_out[...]
        pack[unit:, :] = jnp.concatenate(
            [part, jnp.zeros((rows, depth - unit), F32)], axis=1
        ).astype(BF16)


def pack(place, w_out, residual, rows):
    unit, depth = w_out.shape
    shape = (unit + rows, depth)
    return pl.pallas_call(
        pack_kernel,
        out_shape=[jax.ShapeDtypeStruct(shape, BF16)] + [pltpu.HBM(shape, BF16)] * (NX - 1),
        grid=(1,),
        in_specs=[pl.BlockSpec(memory_space=pltpu.SMEM), HBM, HBM],
        out_specs=[whole(shape)] * NX,
        scratch_shapes=buffers_for((w_out, residual)),
        compiler_params=pltpu.CompilerParams(vmem_limit_bytes=60 << 20),
        name="pack",
    )(place, w_out, residual)


def project_kernel(place, attended, *refs):
    packs, (partial, residual) = refs[:NX], refs[NX:]
    depth = attended.shape[-1]
    value = attended[...].reshape(-1, depth)
    unit = packs[0].shape[0] - residual.shape[0]
    products = [
        lax.dot_general(
            value, pack[:unit, :], (((1,), (1,)), ((), ())), preferred_element_type=F32
        )
        for pack in packs
    ]
    rows = [pack[unit:, :].astype(F32)[:, :unit] for pack in packs]
    x = place[2]

    def order(parts):
        blocks = []
        for i in range(NX):
            away = lax.rem(x - i + NX, NX)
            block = parts[NX - 1]
            for shift in range(NX - 1):
                block = jnp.where(away == shift, parts[shift], block)
            blocks.append(block)
        return jnp.concatenate(blocks, axis=1).astype(BF16)

    wide = order(products)
    count, part = residual.shape
    for y in range(NY):
        for core in range(NC):
            partial[y * NC + core] = wide[
                y * count : (y + 1) * count, core * part : (core + 1) * part
            ]
    wide = order(rows)
    residual[...] = jnp.where(place[1] == 0, wide[:, :part], wide[:, part:])


def project(place, attended, packs):
    _, rows, depth = attended.shape
    unit = packs[0].shape[0] - NC * rows
    shape = (NC * rows, NX * unit // NC)
    vmem = pl.BlockSpec(memory_space=pltpu.VMEM)
    return pl.pallas_call(
        project_kernel,
        out_shape=(
            jax.ShapeDtypeStruct((NY * NC, *shape), BF16),
            jax.ShapeDtypeStruct(shape, BF16),
        ),
        in_specs=[pl.BlockSpec(memory_space=pltpu.SMEM)] + [vmem] * (1 + NX),
        out_specs=(vmem, vmem),
        compiler_params=pltpu.CompilerParams(vmem_limit_bytes=32 << 20),
        cost_estimate=pl.CostEstimate(
            flops=2 * NZ * rows * depth * NX * unit, bytes_accessed=2 << 20, transcendentals=0
        ),
        name="project",
    )(place, attended, *packs)


def expert_kernel(
    place, own, other, gate_w, up_w, router_w, ids, act, gate_sum, up_sum, route_sum, squares
):
    step = pl.program_id(0)
    width = own.shape[-1]

    def products(state):
        gate = up = route = square = 0.0
        for block in range(state.shape[1]):
            hidden = state[:, block].reshape(-1, width)
            gate += jnp.dot(
                hidden, gate_w[:, block].reshape(width, -1), preferred_element_type=F32
            )
            up += jnp.dot(hidden, up_w[:, block].reshape(width, -1), preferred_element_type=F32)
            route += lax.dot_general(
                hidden, router_w[block], (((1,), (1,)), ((), ())), preferred_element_type=F32
            )
            wide = hidden.astype(F32)
            for start in range(0, width, 128):
                piece = wide[:, start : start + 128]
                square += piece * piece
        return gate, up, route, square

    @pl.when(step == 0)
    def _():
        gate_sum[...], up_sum[...], route_sum[...], squares[...] = products(own)

    @pl.when(step == 1)
    def _():
        gate, up, route, square = products(other)
        square += squares[...]
        mean = jnp.sum(square, axis=1, keepdims=True) / (width * NZ * NC)
        scale = lax.rsqrt(mean + EPS)
        logits = (route + route_sum[...]) * scale
        lanes = lax.broadcasted_iota(jnp.int32, logits.shape, 1)
        first = ids[:, 0:1]
        second = ids[:, 1:2]
        first_logit = jnp.sum(jnp.where(lanes == first, logits, 0.0), axis=1, keepdims=True)
        second_logit = jnp.sum(jnp.where(lanes == second, logits, 0.0), axis=1, keepdims=True)
        expert = place[0]
        is_first = first == expert
        gap = second_logit - first_logit
        weight = 1.0 / (1.0 + jnp.exp(jnp.where(is_first, gap, -gap)))
        weight = jnp.where(is_first | (second == expert), weight, 0.0)
        gated = (gate + gate_sum[...]) * scale
        value = jax.nn.silu(gated) * ((up + up_sum[...]) * scale)
        act[...] = (weight * value).astype(BF16)


def experts(place, own, other, gate_w, up_w, router_w, ids):
    _, _, rows, width = own.shape
    total = NXY * rows
    hidden_units = gate_w.shape[-1]
    part = NX // NC
    unit = width // part
    count = router_w.shape[1]

    def half(s, p):
        return p[1] + s - 2 * p[1] * s

    weights = pl.BlockSpec(
        (part, NZ, unit, hidden_units), lambda s, p: (half(s, p), 0, 0, 0)
    )
    return pl.pallas_call(
        expert_kernel,
        out_shape=jax.ShapeDtypeStruct((total, hidden_units), BF16),
        grid_spec=pltpu.PrefetchScalarGridSpec(
            num_scalar_prefetch=1,
            grid=(NC,),
            in_specs=[
                whole(own.shape),
                whole(other.shape),
                weights,
                weights,
                pl.BlockSpec((NZ, count, width), lambda s, p: (0, 0, half(s, p))),
                whole(ids.shape),
            ],
            out_specs=whole((total, hidden_units)),
            scratch_shapes=[
                pltpu.VMEM((total, hidden_units), F32),
                pltpu.VMEM((total, hidden_units), F32),
                pltpu.VMEM((total, count), F32),
                pltpu.VMEM((total, 128), F32),
            ],
        ),
        compiler_params=pltpu.CompilerParams(
            dimension_semantics=("arbitrary",), vmem_limit_bytes=32 << 20
        ),
        cost_estimate=pl.CostEstimate(
            flops=4 * total * width * NZ * 2 * hidden_units,
            bytes_accessed=10 << 20,
            transcendentals=total * hidden_units,
        ),
        name="experts",
    )(
        place,
        own,
        other,
        gate_w.reshape(NX, NZ, unit, hidden_units),
        up_w.reshape(NX, NZ, unit, hidden_units),
        router_w,
        ids,
    )


def down_kernel(place, mine, theirs, w_mine, w_theirs, out):
    total = jnp.dot(mine[...], w_mine[...], preferred_element_type=F32)
    total += jnp.dot(theirs[...], w_theirs[...], preferred_element_type=F32)
    out[0] = total.astype(BF16).reshape(out.shape[1:])


def down(place, mine, theirs, w_mine, w_theirs):
    total, units = mine.shape
    rows = total // NXY
    width = w_theirs.shape[1] // NX
    return pl.pallas_call(
        down_kernel,
        out_shape=pltpu.HBM((NX, NXY, rows, width), BF16),
        grid_spec=pltpu.PrefetchScalarGridSpec(
            num_scalar_prefetch=1,
            grid=(NX,),
            in_specs=[
                whole(mine.shape),
                whole(theirs.shape),
                pl.BlockSpec((units, width), lambda x, p: (0, p[1] * NX + x)),
                pl.BlockSpec((units, width), lambda x, p: (0, x)),
            ],
            out_specs=pl.BlockSpec((1, NXY, rows, width), lambda x, p: (x, 0, 0, 0)),
        ),
        compiler_params=pltpu.CompilerParams(
            dimension_semantics=("arbitrary",), vmem_limit_bytes=32 << 20
        ),
        cost_estimate=pl.CostEstimate(
            flops=4 * total * units * width * NX, bytes_accessed=5 << 20, transcendentals=0
        ),
        name="down",
    )(place, mine, theirs, w_mine, w_theirs)


def head_kernel(own, other, w_own, w_other, below, out):
    width = own.shape[-1]
    vocab = w_own.shape[1]
    near = own[...].reshape(-1, width)
    far = other[...].reshape(-1, width)
    logits = jnp.dot(near, w_own[...], preferred_element_type=F32)
    logits += jnp.dot(far, w_other[...], preferred_element_type=F32)
    square = jnp.zeros((near.shape[0], 128), F32)
    for part in (near.astype(F32), far.astype(F32)):
        for start in range(0, width, 128):
            piece = part[:, start : start + 128]
            square += piece * piece
    square = jnp.sum(square, axis=1, keepdims=True)
    high = square.astype(BF16).astype(F32)
    lanes = lax.broadcasted_iota(jnp.int32, (near.shape[0], 128), 1)
    extra = jnp.where(lanes == 0, high, jnp.where(lanes == 1, square - high, 0.0))
    count = near.shape[0] // NX
    out[:, :count, :vocab] = logits.astype(BF16).reshape(NX, count, vocab)
    out[:, :count, vocab:] = extra.astype(BF16).reshape(NX, count, 128)
    out[:, count:, :] = below[...]


def head(own, other, w_own, w_other, below):
    vocab = w_own.shape[1]
    total = own.shape[0] * own.shape[1] * own.shape[2]
    rows = total // NX + below.shape[1]
    return pl.pallas_call(
        head_kernel,
        out_shape=pltpu.HBM((NX, rows, vocab + 128), BF16),
        compiler_params=pltpu.CompilerParams(vmem_limit_bytes=32 << 20),
        cost_estimate=pl.CostEstimate(
            flops=4 * total * own.shape[3] * vocab, bytes_accessed=4 << 20, transcendentals=0
        ),
        name="head",
    )(own, other, w_own, w_other, below)


def finish_kernel(place, parts, token, stats):
    count = token.shape[0]
    vocab = parts.shape[2] - 128
    total = jnp.sum(parts[:, :count, :].astype(F32), axis=0)
    square = jnp.sum(total[:, vocab:], axis=1, keepdims=True)
    logits = total[:, :vocab] * lax.rsqrt(square / place[1] + EPS)
    top = jnp.max(logits, axis=1, keepdims=True)
    summed = jnp.sum(jnp.exp(logits - top), axis=1, keepdims=True)
    slice_width = vocab // NX
    local = token[...] - place[0] * slice_width
    block = NZ * NY * NC * slice_width
    lanes = lax.broadcasted_iota(jnp.int32, logits.shape, 1)
    entry = (lanes // slice_width) * block + lanes % slice_width
    chosen = jnp.sum(jnp.where(entry == local, logits, 0.0), axis=1, keepdims=True)
    lane = lax.broadcasted_iota(jnp.int32, stats.shape, 1)
    stats[...] = jnp.where(lane == 0, top, jnp.where(lane == 1, summed, chosen))


def finish(place, parts, token):
    return pl.pallas_call(
        finish_kernel,
        out_shape=jax.ShapeDtypeStruct((token.shape[0], 128), F32),
        in_specs=[
            pl.BlockSpec(memory_space=pltpu.SMEM),
            pl.BlockSpec(memory_space=pltpu.VMEM),
            pl.BlockSpec(memory_space=pltpu.VMEM),
        ],
        compiler_params=pltpu.CompilerParams(vmem_limit_bytes=32 << 20),
        name="finish",
    )(place, parts, token)


def shards(
    queries,
    new_keys,
    new_values,
    k_cache,
    v_cache,
    lengths,
    residual,
    w_out,
    router,
    gain_moe,
    w_gate,
    w_up,
    w_down,
    expert_ids,
    gain_final,
    w_vocab,
    tokens,
    mu,
):
    x, z, y, core = (lax.axis_index(name) for name in ("x", "z", "y", "c"))
    expert = y * NC + core
    place = jnp.stack([expert, core, x]).astype(jnp.int32)
    width_all = gain_moe.shape[0]
    unit = w_out.shape[1]
    total_rows = residual.shape[0]
    part_rows = total_rows // (NX * NY * NC)

    sends = pack(place, w_out.T, residual.T, NC * part_rows)
    *sends, queries = lax.optimization_barrier((*sends, queries))
    packs = [sends[0]]
    for shift in range(1, NX):
        pairs = [(i, (i + shift) % NX) for i in range(NX)]
        packs.append(lax.ppermute(sends[shift], "x", pairs))

    attended = attend(queries, new_keys, new_values, k_cache, v_cache, lengths)
    attended_x = exchange(attended, "z")
    partial_heads, residual_here = project(place, attended_x, packs)
    half = width_all // NC
    slab = half // NX
    pieces = exchange(partial_heads, EX)
    hidden = jnp.sum(pieces.astype(F32), axis=0) + residual_here.astype(F32)
    hidden = hidden.astype(BF16)

    hidden_z = spread(hidden, "z", NZ)
    chunks = [hidden_z[:, k * part_rows : (k + 1) * part_rows] for k in range(NC)]

    early = (*chunks, expert_ids, w_gate, w_up, w_down, router)
    early = lax.optimization_barrier(early)
    chunks = list(early[:NC])
    expert_ids, w_gate, w_up, w_down, router = early[NC:]
    own = [spread(chunks[0], XY, NXY)]
    order = expert_ids.reshape(NXY, NC, part_rows, 2).transpose(1, 0, 2, 3)
    order = order.reshape(NC, -1, 2)
    gain_col = gain_moe[:, None]
    router_g = (router.astype(F32) * gain_col).astype(BF16)
    router_z = router_g.T.reshape(-1, NX, NZ, unit).transpose(2, 0, 1, 3)
    router_z = router_z.reshape(NZ, -1, NX * unit)
    gate_g = (w_gate[0].astype(F32) * gain_col).astype(BF16)
    up_g = (w_up[0].astype(F32) * gain_col).astype(BF16)
    down_sent = lax.dynamic_slice_in_dim(w_down[0], (1 - core) * half, half, axis=1)
    down_other = swap_cores(down_sent)
    ready = (own[0], chunks[1], gate_g, up_g, router_z, order, down_other)
    ready = lax.optimization_barrier(ready)
    own[0], chunks[1], gate_g, up_g, router_z, order, down_other = ready
    own.append(spread(chunks[1], XY, NXY))
    other = []
    sums = []
    for k in range(NC):
        other.append(swap_cores(own[k]))
        act = experts(place, own[k], other[k], gate_g, up_g, router_z, order[k])
        sent = down(place, act, swap_cores(act), w_down[0], down_other)
        if k == 0:
            own[1], sent = lax.optimization_barrier((own[1], sent))
        sent = sent.reshape(NXY, NZ // NC, part_rows, slab)
        sums.append(jnp.sum(exchange(sent, XY).astype(F32), axis=0).astype(BF16))
    sums = jnp.stack(sums, axis=1).reshape(NZ, part_rows, slab)
    sums, w_vocab = lax.optimization_barrier((sums, w_vocab))
    vocab_rows = w_vocab.reshape(NC, NX, slab, -1)
    vocab_parts = []
    for shift in range(NX):
        part = lax.dynamic_index_in_dim(vocab_rows, (x + shift) % NX, 1, keepdims=False)
        if shift:
            part = lax.ppermute(part, "x", [(i, (i + shift) % NX) for i in range(NX)])
        vocab_parts.append(part)
    gain_slab = gain_final.reshape(NC, NX, slab)
    gain_slab = lax.dynamic_index_in_dim(gain_slab, x, 1, keepdims=False)[:, :, None]
    columns = []
    for i in range(NX):
        away = (x - i) % NX
        part = vocab_parts[NX - 1]
        for shift in range(NX - 1):
            part = jnp.where(away == shift, vocab_parts[shift], part)
        columns.append((part.astype(F32) * gain_slab).astype(BF16))
    head_w = jnp.concatenate(columns, axis=2)
    head_own = lax.dynamic_index_in_dim(head_w, core, 0, keepdims=False)
    head_other = lax.dynamic_index_in_dim(head_w, 1 - core, 0, keepdims=False)

    sums = jnp.sum(exchange(sums, "z").astype(F32), axis=0)

    units = slab // unit
    first_unit = core * (half // unit) + x * units
    here = [lax.dynamic_index_in_dim(a, y * NX + z // 2, 0, keepdims=False) for a in own]
    rows_here = jnp.where(z % 2 == 0, here[0], here[1])
    rows_here = lax.dynamic_slice_in_dim(rows_here, first_unit % NZ, units)
    rows_here = rows_here.reshape(units, part_rows, NX // NC, unit)
    cut = lax.dynamic_index_in_dim(rows_here, x // NC, 2, keepdims=False)
    hidden_here = cut.transpose(1, 0, 2).reshape(part_rows, slab).astype(F32)
    moved = (hidden_here + sums).astype(BF16)

    moved_z = spread(moved, "z", NZ)
    moved_z, head_own, head_other = lax.optimization_barrier((moved_z, head_own, head_other))
    final_own = spread(moved_z, "y", NY).reshape(NY, NZ, part_rows, slab)
    final_other = swap_cores(final_own)
    count = total_rows // NX

    own_rows = total_rows // (NX * NZ * NY * NC)
    size = (NX, 1, own_rows, slab)
    start = (0, z, expert * own_rows, 0)
    near = lax.dynamic_slice(final_own, start, size)
    far = lax.dynamic_slice(final_other, start, size)
    low = jnp.where(core == 0, near, far)
    high = jnp.where(core == 0, far, near)
    vocab = head_own.shape[1]
    rows_out = jnp.concatenate([low, high], axis=1).reshape(NX, -1, vocab)
    below = jnp.pad(rows_out, ((0, 0), (0, 16 - rows_out.shape[1]), (0, 128)))
    partial = head(final_own, final_other, head_own, head_other, below)
    parts = exchange(partial, "x")
    hidden_out = parts[:, count : count + rows_out.shape[1], :vocab]
    hidden_out = hidden_out.reshape(NX, NC, own_rows, slab).transpose(2, 1, 0, 3)
    hidden_out = hidden_out.reshape(own_rows, width_all)

    token = lax.dynamic_slice_in_dim(tokens, x * count, count)[:, None]
    where = jnp.stack([z * (NY * NC) + expert, jnp.int32(width_all)]).astype(jnp.int32)
    stats = finish(where, parts, token)
    flat = stats[:, :4].reshape(-1, own_rows * 4)
    flat = jnp.pad(flat, ((0, 0), (0, 128 - own_rows * 4)))
    got = exchange(flat, ("z", "y", "c"))[:, : own_rows * 4].reshape(-1, own_rows, 4)
    top = jnp.max(got[:, :, 0], axis=0)
    summed_all = jnp.sum(got[:, :, 1] * jnp.exp(got[:, :, 0] - top[None]), axis=0)
    chosen = jnp.sum(got[:, :, 2], axis=0)
    surprise = (top + jnp.log(summed_all) - chosen) / LOG_TWO
    mu_next = mu - RATE * (surprise - TARGET)
    return (hidden_out, surprise, mu_next)


def solution(mesh):
    fine = Mesh(mesh.devices.reshape(NX, NZ, NY, NC), ALL)
    dp = ("x", "z")
    return jax.shard_map(
        shards,
        mesh=fine,
        in_specs=(
            P(dp, EX),
            P(dp, EX),
            P(dp, EX),
            P(dp, EX, None, None),
            P(dp, EX, None, None),
            P(dp),
            P(None, dp),
            P(EX, dp),
            P(),
            P(),
            P(EX, None, dp),
            P(EX, None, dp),
            P(EX, dp, None),
            P(),
            P(),
            P(None, ALL),
            P(),
            P(ALL),
        ),
        out_specs=(P(ALL, None), P(ALL), P(ALL)),
        check_vma=False,
    )
```

```python
import jax
import jax.numpy as jnp
from jax import lax
from jax.experimental import pallas as pl
from jax.experimental.pallas import tpu as pltpu
from jax.sharding import Mesh
from jax.sharding import PartitionSpec as P

EPS = 1e-05
TARGET = 5.0
RATE = 0.1
LOG_TWO = 0.6931471805599453
F32 = jnp.float32
BF16 = jnp.bfloat16
NX, NZ, NY, NC = 4, 8, 4, 2
NXY = NX * NY
XY = ("x", "y")
EX = ("y", "c")
ALL = ("x", "z", "y", "c")


def whole(shape):
    return pl.BlockSpec(shape, lambda *_: (0,) * len(shape))


HBM = pl.BlockSpec(memory_space=pltpu.HBM)


def fetch(sources, buffers, sems):
    copies = [
        pltpu.make_async_copy(source, buffer, sems.at[i])
        for i, (source, buffer) in enumerate(zip(sources, buffers))
    ]
    for copy in copies:
        copy.start()
    for copy in copies:
        copy.wait()


def buffers_for(arrays):
    return [pltpu.VMEM(a.shape, a.dtype) for a in arrays] + [
        pltpu.SemaphoreType.DMA((len(arrays),))
    ]


def swap_cores(value):
    return lax.ppermute(value, "c", [(0, 1), (1, 0)])


def exchange(value, axes):
    return lax.all_to_all(value, axes, split_axis=0, concat_axis=0, tiled=True)


def spread(value, axes, count):
    return exchange(jnp.broadcast_to(value[None], (count,) + value.shape), axes)


def attend_kernel(lengths, *refs):
    out = refs[5]
    fetch(refs[:5], refs[6:11], refs[11])
    queries, new_keys, new_values, k_cache, v_cache = refs[6:11]
    rows, _, span, width = k_cache.shape
    group = queries.shape[1] // width
    total = group * rows
    query = jnp.concatenate(
        [queries[:, h * width : (h + 1) * width] for h in range(group)], axis=0
    )
    scale = width ** (-0.5)
    keys = k_cache[...].reshape(rows * span, width)
    scores = (
        lax.dot_general(query, keys, (((1,), (1,)), ((), ())), preferred_element_type=F32) * scale
    )
    fresh_key = jnp.concatenate([new_keys[...].astype(F32)] * group, axis=0)
    fresh = jnp.sum(query.astype(F32) * fresh_key, axis=1, keepdims=True) * scale
    request = lax.broadcasted_iota(jnp.int32, (total, 1), 0) % rows
    first = request * span
    last = first
    for r in range(rows):
        last = jnp.where(request == r, r * span + lengths[r], last)
    column = lax.broadcasted_iota(jnp.int32, scores.shape, 1)
    scores = jnp.where((column >= first) & (column < last), scores, -1e30)
    top = jnp.maximum(jnp.max(scores, axis=1, keepdims=True), fresh)
    part = jnp.exp(scores - top)
    part_fresh = jnp.exp(fresh - top)
    sums = jnp.sum(part, axis=1, keepdims=True) + part_fresh
    weight = (part / sums).astype(BF16)
    weight_fresh = (part_fresh / sums).astype(BF16).astype(F32)
    values = v_cache[...].reshape(rows * span, width)
    result = jnp.dot(weight, values, preferred_element_type=F32)
    fresh_value = jnp.concatenate([new_values[...].astype(F32)] * group, axis=0)
    result = (result + weight_fresh * fresh_value).astype(BF16)
    wide = jnp.concatenate([result[h * rows : (h + 1) * rows] for h in range(group)], axis=1)
    for z in range(out.shape[0]):
        out[z] = wide


def attend(queries, new_keys, new_values, k_cache, v_cache, lengths):
    rows, width = queries.shape
    arrays = (queries, new_keys, new_values, k_cache, v_cache)
    return pl.pallas_call(
        attend_kernel,
        out_shape=pltpu.HBM((NZ, rows, width), BF16),
        grid=(1,),
        in_specs=[pl.BlockSpec(memory_space=pltpu.SMEM)] + [HBM] * len(arrays),
        out_specs=whole((NZ, rows, width)),
        scratch_shapes=buffers_for(arrays),
        compiler_params=pltpu.CompilerParams(vmem_limit_bytes=60 << 20),
        cost_estimate=pl.CostEstimate(flops=2 << 34, bytes_accessed=2 << 20, transcendentals=0),
        name="attend",
    )(lengths, *arrays)


def pack_kernel(place, *refs):
    packs = refs[2 : 2 + NX]
    w_out, residual, sems = refs[2 + NX :]
    fetch(refs[:2], (w_out, residual), sems)
    unit, depth = w_out.shape
    rows = packs[0].shape[0] - unit
    line = lax.broadcasted_iota(jnp.int32, (NX * rows, residual.shape[1]), 0)
    target = lax.rem(place[2] + line // rows, NX)
    wanted = (target * NY + place[0] // NC) * rows + line % rows
    pick = lax.broadcasted_iota(jnp.int32, line.shape, 1) == wanted
    parts = lax.dot_general(
        pick.astype(F32).astype(BF16),
        residual[...],
        (((1,), (1,)), ((), ())),
        preferred_element_type=F32,
    )
    for shift, pack in enumerate(packs):
        part = parts[shift * rows : (shift + 1) * rows, :]
        pack[:unit, :] = w_out[...]
        pack[unit:, :] = jnp.concatenate(
            [part, jnp.zeros((rows, depth - unit), F32)], axis=1
        ).astype(BF16)


def pack(place, w_out, residual, rows):
    unit, depth = w_out.shape
    shape = (unit + rows, depth)
    return pl.pallas_call(
        pack_kernel,
        out_shape=[jax.ShapeDtypeStruct(shape, BF16)] + [pltpu.HBM(shape, BF16)] * (NX - 1),
        grid=(1,),
        in_specs=[pl.BlockSpec(memory_space=pltpu.SMEM), HBM, HBM],
        out_specs=[whole(shape)] * NX,
        scratch_shapes=buffers_for((w_out, residual)),
        compiler_params=pltpu.CompilerParams(vmem_limit_bytes=60 << 20),
        name="pack",
    )(place, w_out, residual)


def project_kernel(place, attended, *refs):
    packs, (partial, residual) = refs[:NX], refs[NX:]
    depth = attended.shape[-1]
    value = attended[...].reshape(-1, depth)
    unit = packs[0].shape[0] - residual.shape[0]
    products = [
        lax.dot_general(
            value, pack[:unit, :], (((1,), (1,)), ((), ())), preferred_element_type=F32
        )
        for pack in packs
    ]
    rows = [pack[unit:, :].astype(F32)[:, :unit] for pack in packs]
    x = place[2]

    def order(parts):
        blocks = []
        for i in range(NX):
            away = lax.rem(x - i + NX, NX)
            block = parts[NX - 1]
            for shift in range(NX - 1):
                block = jnp.where(away == shift, parts[shift], block)
            blocks.append(block)
        return jnp.concatenate(blocks, axis=1).astype(BF16)

    wide = order(products)
    count, part = residual.shape
    for y in range(NY):
        for core in range(NC):
            partial[y * NC + core] = wide[
                y * count : (y + 1) * count, core * part : (core + 1) * part
            ]
    wide = order(rows)
    residual[...] = jnp.where(place[1] == 0, wide[:, :part], wide[:, part:])


def project(place, attended, packs):
    _, rows, depth = attended.shape
    unit = packs[0].shape[0] - NC * rows
    shape = (NC * rows, NX * unit // NC)
    vmem = pl.BlockSpec(memory_space=pltpu.VMEM)
    return pl.pallas_call(
        project_kernel,
        out_shape=(
            jax.ShapeDtypeStruct((NY * NC, *shape), BF16),
            jax.ShapeDtypeStruct(shape, BF16),
        ),
        in_specs=[pl.BlockSpec(memory_space=pltpu.SMEM)] + [vmem] * (1 + NX),
        out_specs=(vmem, vmem),
        compiler_params=pltpu.CompilerParams(vmem_limit_bytes=32 << 20),
        cost_estimate=pl.CostEstimate(
            flops=2 * NZ * rows * depth * NX * unit, bytes_accessed=2 << 20, transcendentals=0
        ),
        name="project",
    )(place, attended, *packs)


def expert_kernel(
    place, own, other, gate_w, up_w, router_w, ids, act, gate_sum, up_sum, route_sum, squares
):
    step = pl.program_id(0)
    width = own.shape[-1]

    def products(state):
        gate = up = route = square = 0.0
        for block in range(state.shape[1]):
            hidden = state[:, block].reshape(-1, width)
            gate += jnp.dot(
                hidden, gate_w[:, block].reshape(width, -1), preferred_element_type=F32
            )
            up += jnp.dot(hidden, up_w[:, block].reshape(width, -1), preferred_element_type=F32)
            route += lax.dot_general(
                hidden, router_w[block], (((1,), (1,)), ((), ())), preferred_element_type=F32
            )
            wide = hidden.astype(F32)
            for start in range(0, width, 128):
                piece = wide[:, start : start + 128]
                square += piece * piece
        return gate, up, route, square

    @pl.when(step == 0)
    def _():
        gate_sum[...], up_sum[...], route_sum[...], squares[...] = products(own)

    @pl.when(step == 1)
    def _():
        gate, up, route, square = products(other)
        square += squares[...]
        mean = jnp.sum(square, axis=1, keepdims=True) / (width * NZ * NC)
        scale = lax.rsqrt(mean + EPS)
        logits = (route + route_sum[...]) * scale
        lanes = lax.broadcasted_iota(jnp.int32, logits.shape, 1)
        first = ids[:, 0:1]
        second = ids[:, 1:2]
        first_logit = jnp.sum(jnp.where(lanes == first, logits, 0.0), axis=1, keepdims=True)
        second_logit = jnp.sum(jnp.where(lanes == second, logits, 0.0), axis=1, keepdims=True)
        expert = place[0]
        is_first = first == expert
        gap = second_logit - first_logit
        weight = 1.0 / (1.0 + jnp.exp(jnp.where(is_first, gap, -gap)))
        weight = jnp.where(is_first | (second == expert), weight, 0.0)
        gated = (gate + gate_sum[...]) * scale
        value = jax.nn.silu(gated) * ((up + up_sum[...]) * scale)
        act[...] = (weight * value).astype(BF16)


def experts(place, own, other, gate_w, up_w, router_w, ids):
    _, _, rows, width = own.shape
    total = NXY * rows
    hidden_units = gate_w.shape[-1]
    part = NX // NC
    unit = width // part
    count = router_w.shape[1]

    def half(s, p):
        return p[1] + s - 2 * p[1] * s

    weights = pl.BlockSpec(
        (part, NZ, unit, hidden_units), lambda s, p: (half(s, p), 0, 0, 0)
    )
    return pl.pallas_call(
        expert_kernel,
        out_shape=jax.ShapeDtypeStruct((total, hidden_units), BF16),
        grid_spec=pltpu.PrefetchScalarGridSpec(
            num_scalar_prefetch=1,
            grid=(NC,),
            in_specs=[
                whole(own.shape),
                whole(other.shape),
                weights,
                weights,
                pl.BlockSpec((NZ, count, width), lambda s, p: (0, 0, half(s, p))),
                whole(ids.shape),
            ],
            out_specs=whole((total, hidden_units)),
            scratch_shapes=[
                pltpu.VMEM((total, hidden_units), F32),
                pltpu.VMEM((total, hidden_units), F32),
                pltpu.VMEM((total, count), F32),
                pltpu.VMEM((total, 128), F32),
            ],
        ),
        compiler_params=pltpu.CompilerParams(
            dimension_semantics=("arbitrary",), vmem_limit_bytes=32 << 20
        ),
        cost_estimate=pl.CostEstimate(
            flops=4 * total * width * NZ * 2 * hidden_units,
            bytes_accessed=10 << 20,
            transcendentals=total * hidden_units,
        ),
        name="experts",
    )(
        place,
        own,
        other,
        gate_w.reshape(NX, NZ, unit, hidden_units),
        up_w.reshape(NX, NZ, unit, hidden_units),
        router_w,
        ids,
    )


def down_kernel(place, mine, theirs, w_mine, w_theirs, out):
    total = jnp.dot(mine[...], w_mine[...], preferred_element_type=F32)
    total += jnp.dot(theirs[...], w_theirs[...], preferred_element_type=F32)
    out[0] = total.astype(BF16).reshape(out.shape[1:])


def down(place, mine, theirs, w_mine, w_theirs):
    total, units = mine.shape
    rows = total // NXY
    width = w_theirs.shape[1] // NX
    return pl.pallas_call(
        down_kernel,
        out_shape=pltpu.HBM((NX, NXY, rows, width), BF16),
        grid_spec=pltpu.PrefetchScalarGridSpec(
            num_scalar_prefetch=1,
            grid=(NX,),
            in_specs=[
                whole(mine.shape),
                whole(theirs.shape),
                pl.BlockSpec((units, width), lambda x, p: (0, p[1] * NX + x)),
                pl.BlockSpec((units, width), lambda x, p: (0, x)),
            ],
            out_specs=pl.BlockSpec((1, NXY, rows, width), lambda x, p: (x, 0, 0, 0)),
        ),
        compiler_params=pltpu.CompilerParams(
            dimension_semantics=("arbitrary",), vmem_limit_bytes=32 << 20
        ),
        cost_estimate=pl.CostEstimate(
            flops=4 * total * units * width * NX, bytes_accessed=5 << 20, transcendentals=0
        ),
        name="down",
    )(place, mine, theirs, w_mine, w_theirs)


def head_kernel(own, other, w_own, w_other, below, out):
    width = own.shape[-1]
    vocab = w_own.shape[1]
    near = own[...].reshape(-1, width)
    far = other[...].reshape(-1, width)
    logits = jnp.dot(near, w_own[...], preferred_element_type=F32)
    logits += jnp.dot(far, w_other[...], preferred_element_type=F32)
    square = jnp.zeros((near.shape[0], 128), F32)
    for part in (near.astype(F32), far.astype(F32)):
        for start in range(0, width, 128):
            piece = part[:, start : start + 128]
            square += piece * piece
    square = jnp.sum(square, axis=1, keepdims=True)
    high = square.astype(BF16).astype(F32)
    lanes = lax.broadcasted_iota(jnp.int32, (near.shape[0], 128), 1)
    extra = jnp.where(lanes == 0, high, jnp.where(lanes == 1, square - high, 0.0))
    count = near.shape[0] // NX
    out[:, :count, :vocab] = logits.astype(BF16).reshape(NX, count, vocab)
    out[:, :count, vocab:] = extra.astype(BF16).reshape(NX, count, 128)
    out[:, count:, :] = below[...]


def head(own, other, w_own, w_other, below):
    vocab = w_own.shape[1]
    total = own.shape[0] * own.shape[1] * own.shape[2]
    rows = total // NX + below.shape[1]
    return pl.pallas_call(
        head_kernel,
        out_shape=pltpu.HBM((NX, rows, vocab + 128), BF16),
        compiler_params=pltpu.CompilerParams(vmem_limit_bytes=32 << 20),
        cost_estimate=pl.CostEstimate(
            flops=4 * total * own.shape[3] * vocab, bytes_accessed=4 << 20, transcendentals=0
        ),
        name="head",
    )(own, other, w_own, w_other, below)


def finish_kernel(place, parts, token, stats):
    count = token.shape[0]
    vocab = parts.shape[2] - 128
    total = jnp.sum(parts[:, :count, :].astype(F32), axis=0)
    square = jnp.sum(total[:, vocab:], axis=1, keepdims=True)
    logits = total[:, :vocab] * lax.rsqrt(square / place[1] + EPS)
    top = jnp.max(logits, axis=1, keepdims=True)
    summed = jnp.sum(jnp.exp(logits - top), axis=1, keepdims=True)
    slice_width = vocab // NX
    local = token[...] - place[0] * slice_width
    block = NZ * NY * NC * slice_width
    lanes = lax.broadcasted_iota(jnp.int32, logits.shape, 1)
    entry = (lanes // slice_width) * block + lanes % slice_width
    chosen = jnp.sum(jnp.where(entry == local, logits, 0.0), axis=1, keepdims=True)
    lane = lax.broadcasted_iota(jnp.int32, stats.shape, 1)
    stats[...] = jnp.where(lane == 0, top, jnp.where(lane == 1, summed, chosen))


def finish(place, parts, token):
    return pl.pallas_call(
        finish_kernel,
        out_shape=jax.ShapeDtypeStruct((token.shape[0], 128), F32),
        in_specs=[
            pl.BlockSpec(memory_space=pltpu.SMEM),
            pl.BlockSpec(memory_space=pltpu.VMEM),
            pl.BlockSpec(memory_space=pltpu.VMEM),
        ],
        compiler_params=pltpu.CompilerParams(vmem_limit_bytes=32 << 20),
        name="finish",
    )(place, parts, token)


def shards(
    queries,
    new_keys,
    new_values,
    k_cache,
    v_cache,
    lengths,
    residual,
    w_out,
    router,
    gain_moe,
    w_gate,
    w_up,
    w_down,
    expert_ids,
    gain_final,
    w_vocab,
    tokens,
    mu,
):
    x, z, y, core = (lax.axis_index(name) for name in ("x", "z", "y", "c"))
    expert = y * NC + core
    place = jnp.stack([expert, core, x]).astype(jnp.int32)
    width_all = gain_moe.shape[0]
    unit = w_out.shape[1]
    total_rows = residual.shape[0]
    part_rows = total_rows // (NX * NY * NC)

    sends = pack(place, w_out.T, residual.T, NC * part_rows)
    *sends, queries = lax.optimization_barrier((*sends, queries))
    packs = [sends[0]]
    for shift in range(1, NX):
        pairs = [(i, (i + shift) % NX) for i in range(NX)]
        packs.append(lax.ppermute(sends[shift], "x", pairs))

    attended = attend(queries, new_keys, new_values, k_cache, v_cache, lengths)
    attended, packs[1], packs[3] = lax.optimization_barrier((attended, packs[1], packs[3]))
    attended_x = exchange(attended, "z")
    partial_heads, residual_here = project(place, attended_x, packs)
    half = width_all // NC
    slab = half // NX
    pieces = exchange(partial_heads, EX)
    hidden = jnp.sum(pieces.astype(F32), axis=0) + residual_here.astype(F32)
    hidden = hidden.astype(BF16)

    hidden_z = spread(hidden, "z", NZ)
    chunks = [hidden_z[:, k * part_rows : (k + 1) * part_rows] for k in range(NC)]

    early = (*chunks, expert_ids, w_gate, w_up, w_down, router)
    early = lax.optimization_barrier(early)
    chunks = list(early[:NC])
    expert_ids, w_gate, w_up, w_down, router = early[NC:]
    own = [spread(chunks[0], XY, NXY)]
    order = expert_ids.reshape(NXY, NC, part_rows, 2).transpose(1, 0, 2, 3)
    order = order.reshape(NC, -1, 2)
    gain_col = gain_moe[:, None]
    router_g = (router.astype(F32) * gain_col).astype(BF16)
    router_z = router_g.T.reshape(-1, NX, NZ, unit).transpose(2, 0, 1, 3)
    router_z = router_z.reshape(NZ, -1, NX * unit)
    gate_g = (w_gate[0].astype(F32) * gain_col).astype(BF16)
    up_g = (w_up[0].astype(F32) * gain_col).astype(BF16)
    down_sent = lax.dynamic_slice_in_dim(w_down[0], (1 - core) * half, half, axis=1)
    down_other = swap_cores(down_sent)
    ready = (own[0], chunks[1], gate_g, up_g, router_z, order, down_other)
    ready = lax.optimization_barrier(ready)
    own[0], chunks[1], gate_g, up_g, router_z, order, down_other = ready
    own.append(spread(chunks[1], XY, NXY))
    other = []
    sums = []
    for k in range(NC):
        other.append(swap_cores(own[k]))
        act = experts(place, own[k], other[k], gate_g, up_g, router_z, order[k])
        sent = down(place, act, swap_cores(act), w_down[0], down_other)
        if k == 0:
            own[1], sent = lax.optimization_barrier((own[1], sent))
        sent = sent.reshape(NXY, NZ // NC, part_rows, slab)
        sums.append(jnp.sum(exchange(sent, XY).astype(F32), axis=0).astype(BF16))
    sums = jnp.stack(sums, axis=1).reshape(NZ, part_rows, slab)
    sums, w_vocab = lax.optimization_barrier((sums, w_vocab))
    vocab_rows = w_vocab.reshape(NC, NX, slab, -1)
    vocab_parts = []
    for shift in range(NX):
        part = lax.dynamic_index_in_dim(vocab_rows, (x + shift) % NX, 1, keepdims=False)
        if shift:
            part = lax.ppermute(part, "x", [(i, (i + shift) % NX) for i in range(NX)])
        vocab_parts.append(part)
    gain_slab = gain_final.reshape(NC, NX, slab)
    gain_slab = lax.dynamic_index_in_dim(gain_slab, x, 1, keepdims=False)[:, :, None]
    columns = []
    for i in range(NX):
        away = (x - i) % NX
        part = vocab_parts[NX - 1]
        for shift in range(NX - 1):
            part = jnp.where(away == shift, vocab_parts[shift], part)
        columns.append((part.astype(F32) * gain_slab).astype(BF16))
    head_w = jnp.concatenate(columns, axis=2)
    head_own = lax.dynamic_index_in_dim(head_w, core, 0, keepdims=False)
    head_other = lax.dynamic_index_in_dim(head_w, 1 - core, 0, keepdims=False)

    sums = jnp.sum(exchange(sums, "z").astype(F32), axis=0)

    units = slab // unit
    first_unit = core * (half // unit) + x * units
    here = [lax.dynamic_index_in_dim(a, y * NX + z // 2, 0, keepdims=False) for a in own]
    rows_here = jnp.where(z % 2 == 0, here[0], here[1])
    rows_here = lax.dynamic_slice_in_dim(rows_here, first_unit % NZ, units)
    rows_here = rows_here.reshape(units, part_rows, NX // NC, unit)
    cut = lax.dynamic_index_in_dim(rows_here, x // NC, 2, keepdims=False)
    hidden_here = cut.transpose(1, 0, 2).reshape(part_rows, slab).astype(F32)
    moved = (hidden_here + sums).astype(BF16)

    moved_z = spread(moved, "z", NZ)
    moved_z, head_own, head_other = lax.optimization_barrier((moved_z, head_own, head_other))
    final_own = spread(moved_z, "y", NY).reshape(NY, NZ, part_rows, slab)
    final_other = swap_cores(final_own)
    count = total_rows // NX

    own_rows = total_rows // (NX * NZ * NY * NC)
    size = (NX, 1, own_rows, slab)
    start = (0, z, expert * own_rows, 0)
    near = lax.dynamic_slice(final_own, start, size)
    far = lax.dynamic_slice(final_other, start, size)
    low = jnp.where(core == 0, near, far)
    high = jnp.where(core == 0, far, near)
    vocab = head_own.shape[1]
    rows_out = jnp.concatenate([low, high], axis=1).reshape(NX, -1, vocab)
    below = jnp.pad(rows_out, ((0, 0), (0, 16 - rows_out.shape[1]), (0, 128)))
    partial = head(final_own, final_other, head_own, head_other, below)
    parts = exchange(partial, "x")
    hidden_out = parts[:, count : count + rows_out.shape[1], :vocab]
    hidden_out = hidden_out.reshape(NX, NC, own_rows, slab).transpose(2, 1, 0, 3)
    hidden_out = hidden_out.reshape(own_rows, width_all)

    token = lax.dynamic_slice_in_dim(tokens, x * count, count)[:, None]
    where = jnp.stack([z * (NY * NC) + expert, jnp.int32(width_all)]).astype(jnp.int32)
    stats = finish(where, parts, token)
    flat = stats[:, :4].reshape(-1, own_rows * 4)
    flat = jnp.pad(flat, ((0, 0), (0, 128 - own_rows * 4)))
    got = exchange(flat, ("z", "y", "c"))[:, : own_rows * 4].reshape(-1, own_rows, 4)
    top = jnp.max(got[:, :, 0], axis=0)
    summed_all = jnp.sum(got[:, :, 1] * jnp.exp(got[:, :, 0] - top[None]), axis=0)
    chosen = jnp.sum(got[:, :, 2], axis=0)
    surprise = (top + jnp.log(summed_all) - chosen) / LOG_TWO
    mu_next = mu - RATE * (surprise - TARGET)
    return (hidden_out, surprise, mu_next)


def solution(mesh):
    fine = Mesh(mesh.devices.reshape(NX, NZ, NY, NC), ALL)
    dp = ("x", "z")
    return jax.shard_map(
        shards,
        mesh=fine,
        in_specs=(
            P(dp, EX),
            P(dp, EX),
            P(dp, EX),
            P(dp, EX, None, None),
            P(dp, EX, None, None),
            P(dp),
            P(None, dp),
            P(EX, dp),
            P(),
            P(),
            P(EX, None, dp),
            P(EX, None, dp),
            P(EX, dp, None),
            P(),
            P(),
            P(None, ALL),
            P(),
            P(ALL),
        ),
        out_specs=(P(ALL, None), P(ALL), P(ALL)),
        check_vma=False,
    )
```
